32 devices in a mesh: patch: 4 (over y, x), dir: 8 (over z, core).
Axes of the slice: x: 2, y: 2, z: 4, core: 2. Of those that a mesh axis runs over, the one named last changes fastest.
Arguments:
- fine_out: bfloat16 [24, 32, 2, 4, 512], P('patch', 'dir'), may hold values from -6 to 6
- interp: bfloat16 [512, 2048], replicated, may hold values from -0.25 to 0.25
- child_phase: float32 [4, 2048], replicated, may hold values from -3.140625 to 3.140625
- fine_ops: float32 [40, 2, 512], replicated, may hold values from -1.2 to 1.2
- parent_ops: float32 [40, 2, 2048], P(None, None, 'dir'), may hold values from -0.6 to 0.6
- fine_src: int32 [24, 32, 32], P('patch'), may hold values from 0 to 767, as said below
- fine_op: int32 [24, 32, 32], P('patch'), may hold values from 0 to 40, as said below
- parent_src: int32 [12, 16, 32], P('patch'), may hold values from 0 to 191, as said below
- parent_op: int32 [12, 16, 32], P('patch'), may hold values from 0 to 40, as said below
Outputs:
- fine_in: float32 [24, 32, 2, 4, 512], P('patch', 'dir')
The draws below stay inside these ranges and needn't reach their ends.
Inputs may be any that keep to these rules, and one draw needn't show every extreme that they name: `fine_src`: A slot with op id 40 is padding and names the box itself. Every other slot names a distinct box at most 3 rows and 3 columns away, not adjacent to the box, whose parent is adjacent to or equal to the box's parent; its op id is the index of the offset (dr, dc), in order of dr then dc over -3..3, among the offsets with max(|dr|, |dc|) > 1. `fine_op`: as for fine_src. `parent_src`: as for fine_src, on the parent grid. `parent_op`: as for fine_op, on the parent grid.
All inputs are finite; a program needn't handle non-finite values.
Results may differ from the reference program's by a relative error of at most 0.0022.
Values may be sent and summed in bfloat16 or wider, within the bound.
No kernel may reach another device: no remote copies, remote signals or barrier semaphores. Data moves between devices by JAX's collectives and lax.ppermute only.
A program may use at most 128 MiB of HBM per device.

```python
import jax
import jax.numpy as jnp
import numpy as np
from jax import lax

RHS = 4
DF = 512
DP = 2048
OPS = 40
SLOTS = 32
PR = 12
PC = 16
FR = 24
FC = 32


def offset_table():
    pairs = [(first, second) for first in range(-3, 4) for second in range(-3, 4) if max(abs(first), abs(second)) > 1]
    return np.array(pairs, dtype=np.int32)


def build_lists(key, height, across):
    offsets = jnp.asarray(offset_table())
    how_many = offsets.shape[0]
    occ_key, order_key = jax.random.split(key)
    occupied = jax.random.randint(occ_key, (height, across), 0, 10) < 8
    row_at = jnp.arange(height, dtype=jnp.int32)[:, None, None]
    col_at = jnp.arange(across, dtype=jnp.int32)[None, :, None]
    src_row = row_at + offsets[:, 0][None, None, :]
    src_col = col_at + offsets[:, 1][None, None, :]
    inside = (src_row >= 0) & (src_row < height) & (src_col >= 0) & (src_col < across)
    beside = (jnp.abs(src_row // 2 - row_at // 2) <= 1) & (jnp.abs(src_col // 2 - col_at // 2) <= 1)
    safe_row = jnp.clip(src_row, 0, height - 1)
    safe_col = jnp.clip(src_col, 0, across - 1)
    usable = inside & beside & occupied[safe_row, safe_col]
    jitter = jax.random.randint(order_key, (height, across, how_many), 0, 1 << 16) * 64 + jnp.arange(how_many, dtype=jnp.int32)
    ranking = jnp.where(usable, jitter + (1 << 23), jitter)
    _, picked = lax.top_k(ranking, SLOTS)
    picked = picked.astype(jnp.int32)
    chosen = jnp.take_along_axis(usable, picked, axis=2)
    own_box = row_at * across + col_at
    source = jnp.where(chosen, jnp.take_along_axis(safe_row * across + safe_col, picked, axis=2), own_box)
    opcode = jnp.where(chosen, picked, OPS)
    return (source.astype(jnp.int32), opcode.astype(jnp.int32))


def draw_fine_src(key, part):
    return build_lists(jax.random.fold_in(key, 11), FR, FC)[0]


def draw_fine_op(key, part):
    return build_lists(jax.random.fold_in(key, 11), FR, FC)[1]


def draw_parent_src(key, part):
    return build_lists(jax.random.fold_in(key, 23), PR, PC)[0]


def draw_parent_op(key, part):
    return build_lists(jax.random.fold_in(key, 23), PR, PC)[1]


def block_scale(stream_key, dims, cuts, least, high):
    factor_of = 1.0
    for position, parts in cuts:
        steps = jax.random.uniform(jax.random.fold_in(jax.random.fold_in(stream_key, 6), position), (parts,), jnp.float32, least / len(cuts), high / len(cuts))
        factor_of = factor_of * jnp.repeat(jnp.exp(steps), dims[position] // parts).reshape((-1,) + (1,) * (len(dims) - 1 - position))
    return factor_of


def gaussian(stream_key, shape, deviation, most, shards=(), kind=jnp.bfloat16):
    loudness = block_scale(stream_key, shape, shards, -0.22, 0.18) if shards else 1.0
    entries = jax.random.normal(stream_key, shape, jnp.float32) * deviation * loudness
    return jnp.minimum(jnp.maximum(entries, -most), most).astype(kind)


def setup_inputs(seed: int = 0) -> dict:
    splits = jax.random.split(jax.random.key(seed), 10)
    return {
        "fine_out": gaussian(splits[0], (FR, FC, 2, RHS, DF), 1.0, 6.0, ((0, 4), (1, 8))),
        "interp": gaussian(splits[1], (DF, DP), DF ** -0.5, 0.25),
        "child_phase": jnp.clip(jax.random.uniform(splits[2], (4, DP), jnp.float32, -3.140625, 3.140625), -3.140625, 3.140625),
        "fine_ops": gaussian(splits[3], (OPS, 2, DF), 0.2, 1.2, (), jnp.float32),
        "parent_ops": gaussian(splits[4], (OPS, 2, DP), 0.1, 0.6, ((2, 8),), jnp.float32),
        "fine_src": draw_fine_src(jax.random.fold_in(splits[9], 71), 0),
        "fine_op": draw_fine_op(jax.random.fold_in(splits[9], 71), 0),
        "parent_src": draw_parent_src(jax.random.fold_in(splits[9], 71), 0),
        "parent_op": draw_parent_op(jax.random.fold_in(splits[9], 71), 0),
    }


highest = lax.Precision.HIGHEST


def translate(sources, index, opcode, operators):
    kinds = operators.shape[0]

    def add_slot(running, slot_pair):
        where_from, which_op = slot_pair
        pieces = sources[where_from].astype(jnp.float32)
        one_hot = (which_op[:, None] == jnp.arange(kinds, dtype=jnp.int32)[None, :]).astype(jnp.float32)
        factor = jnp.einsum("bo,ocd->bcd", one_hot, operators, precision=highest)
        cos_part = factor[:, 0, None, :]
        sin_part = factor[:, 1, None, :]
        real_part = cos_part * pieces[:, 0] - sin_part * pieces[:, 1]
        imag_part = cos_part * pieces[:, 1] + sin_part * pieces[:, 0]
        return running + jnp.stack([real_part, imag_part], axis=1), None

    start = jnp.zeros((index.shape[0],) + sources.shape[1:], jnp.float32)
    running, _ = lax.scan(add_slot, start, (index.T, opcode.T))
    return running


def reference(fine_out, interp, child_phase, fine_ops, parent_ops, fine_src, fine_op, parent_src, parent_op):
    fine_rows, fine_cols = fine_out.shape[0], fine_out.shape[1]
    par_rows, par_cols = fine_rows // 2, fine_cols // 2
    cosine = jnp.cos(child_phase).reshape(2, 2, DP)[:, None, :, None, :]
    sine_ab = jnp.sin(child_phase).reshape(2, 2, DP)[:, None, :, None, :]
    interp_wide = interp.astype(jnp.float32)

    def aggregate(strip):
        spread = jnp.dot(strip.reshape(-1, DF).astype(jnp.float32), interp_wide, precision=highest)
        spread = spread.reshape(2, par_cols, 2, 2, RHS, DP)
        real_in = spread[:, :, :, 0]
        imag_in = spread[:, :, :, 1]
        real_sum = jnp.sum(cosine * real_in - sine_ab * imag_in, axis=(0, 2))
        imag_sum = jnp.sum(cosine * imag_in + sine_ab * real_in, axis=(0, 2))
        return jnp.stack([real_sum, imag_sum], axis=1).astype(jnp.bfloat16)

    parent_out = lax.map(aggregate, fine_out.reshape(par_rows, 2, fine_cols, 2, RHS, DF))
    parent_flat = parent_out.reshape(par_rows * par_cols, 2, RHS, DP)

    def parent_row(pair):
        return translate(parent_flat, pair[0], pair[1], parent_ops).astype(jnp.bfloat16)

    parent_in = lax.map(parent_row, (parent_src, parent_op))

    def disaggregate(strip):
        wide_strip = strip.astype(jnp.float32)
        real_in = wide_strip[None, :, None, 0]
        imag_in = wide_strip[None, :, None, 1]
        real_child = cosine * real_in + sine_ab * imag_in
        imag_child = cosine * imag_in - sine_ab * real_in
        child_in = jnp.stack([real_child, imag_child], axis=3).astype(jnp.bfloat16)
        child_in = child_in.reshape(-1, DP).astype(jnp.float32)
        back = jnp.dot(child_in, interp_wide.T, precision=highest) * (DF / DP)
        return back.reshape(2, fine_cols, 2, RHS, DF)

    fine_far = lax.map(disaggregate, parent_in).reshape(fine_rows, fine_cols, 2, RHS, DF)
    fine_flat = fine_out.reshape(fine_rows * fine_cols, 2, RHS, DF)

    def fine_row(pair):
        return translate(fine_flat, pair[0], pair[1], fine_ops)

    fine_near = lax.map(fine_row, (fine_src, fine_op))
    return fine_near + fine_far
```

```python
import functools

import jax
import jax.numpy as jnp
import numpy as np
from jax import lax
from jax.experimental import pallas as pl
from jax.experimental.pallas import tpu as pltpu
from jax.sharding import PartitionSpec as P

CHUNK = 512
HALF = 256


def offset_pairs():
    return [(dr, dc) for dr in range(-3, 4) for dc in range(-3, 4) if max(abs(dr), abs(dc)) > 1]


def class_offsets(row_odd, col_odd):
    picked = []
    for op_id, (dr, dc) in enumerate(offset_pairs()):
        if -2 <= dr + row_odd <= 3 and -2 <= dc + col_odd <= 3:
            picked.append((op_id, dr, dc))
    return picked


def halo_sizes(count):
    return (3, 2) if count % 2 else (2, 2)


def stored_at(rel, count, odd):
    first, second = halo_sizes(count)
    if 0 <= rel < count:
        return rel
    if rel < 0:
        return count + first + rel if odd else count + first + second + rel
    return rel if not odd else rel + first


def storage_index(row, col, rows, cols, row_odd, col_odd, scale):
    first_r, second_r = halo_sizes(rows)
    first_c, second_c = halo_sizes(cols)
    height = (rows + first_r + second_r) * scale
    at_r = stored_at(row // scale, rows, row_odd) * scale + row % scale
    at_c = stored_at(col // scale, cols, col_odd) * scale + col % scale
    base = 0
    for width in (cols * scale, first_c * scale, second_c * scale):
        if at_c < width:
            return base + at_r * width + at_c
        at_c -= width
        base += height * width
    raise ValueError("outside")


def build_tables(rows, cols):
    first_r, second_r = halo_sizes(rows)
    first_c, second_c = halo_sizes(cols)
    boxes = (rows + first_r + second_r) * (cols + first_c + second_c)
    fine_src, par_src, par_op = [], [], []
    for row_odd in range(2):
        for col_odd in range(2):
            row_at, col_at = row_odd * rows, col_odd * cols
            fine = []
            for r in range(2 * rows):
                for c in range(2 * cols):
                    fine.append([
                        storage_index(r + dr, c + dc, rows, cols, row_odd, col_odd, 2)
                        for _, dr, dc in class_offsets(r % 2, c % 2)
                    ])
            src, ops = [], []
            for r in range(rows):
                for c in range(cols):
                    offsets = class_offsets((r + row_at) % 2, (c + col_at) % 2)
                    src.append([
                        storage_index(r + dr, c + dc, rows, cols, row_odd, col_odd, 1)
                        for _, dr, dc in offsets
                    ])
                    ops.append([o for o, _, _ in offsets])
            fine_src.append(fine)
            par_src.append(src)
            par_op.append(ops)
    fine_op = [
        [o for o, _, _ in class_offsets(r % 2, c % 2)]
        for r in range(2 * rows)
        for c in range(2 * cols)
    ]
    as_int = lambda x: np.array(x, np.int32)
    return boxes, as_int(fine_src), as_int(fine_op), as_int(par_src), as_int(par_op)


def pairs(count, first):
    if first:
        return [(i, i ^ 1) for i in range(count) if (i ^ 1) < count]
    found = []
    for i in range(1, count - 1, 2):
        found += [(i, i + 1), (i + 1, i)]
    return found


def exchange(block, axis, unit, count):
    n = lax.axis_size(axis)
    odd = lax.rem(lax.axis_index(axis), 2)
    got = []
    for first, size in zip((True, False), halo_sizes(count)):
        edge = block
        if size < count:
            low = (1 - odd) if first else odd
            edge = lax.dynamic_slice_in_dim(block, low * ((count - size) * unit), size * unit, 0)
        got.append(lax.ppermute(edge, axis, pairs(n, first)))
    return got


def gather_ops(ops, axis):
    n = lax.axis_size(axis)
    at = lax.axis_index(axis)
    bits = n.bit_length() - 1
    block = ops
    for bit in reversed(range(bits)):
        other = lax.ppermute(block, axis, [(i, i ^ (1 << bit)) for i in range(n)])
        mine_first = ((at >> bit) & 1) == 0
        block = jnp.stack([jnp.where(mine_first, block, other), jnp.where(mine_first, other, block)])
    order = tuple(reversed(range(bits)))
    block = block.transpose((bits, bits + 1) + order + (bits + 2,))
    return block.reshape(ops.shape[0], ops.shape[1], n * ops.shape[2])


def kernel(
    rows, cols, sides, boxes,
    fsrc, fop, psrc, pop,
    own, side_a, side_b, interp, phase, fops, pops,
    out, spread, pattern, fine, child, near, acc,
):
    step = pl.program_id(0)
    comps = 2 * sides
    fdirs = own.shape[1]
    lanes = interp.shape[1]
    slots = fsrc.shape[1]
    frows, fcols = 2 * rows, 2 * cols
    height = boxes // (cols + sum(halo_sizes(cols)))
    blocks = (own, side_a, side_b)
    widths = (cols,) + halo_sizes(cols)
    f32, bf16 = jnp.float32, jnp.bfloat16
    sign = jnp.where(lax.broadcasted_iota(jnp.int32, (comps, 1), 0) < sides, -1.0, 1.0).astype(f32)

    def times_i(v):
        return sign * pltpu.roll(v, sides, 0)

    @pl.when(step == 0)
    def _():
        base = 0
        for ref in blocks:
            count = ref.shape[0] // comps
            fine[base : base + count] = ref[...].astype(f32).reshape(count, comps, fdirs)
            base += count
        fine[base] = jnp.zeros((comps, fdirs), f32)
        pattern[boxes] = jnp.zeros((comps, lanes), f32)

    base = 0
    for ref in blocks:
        count = ref.shape[0] // comps
        spread[base : base + count] = jnp.dot(
            ref[...], interp[...], preferred_element_type=f32
        ).reshape(count, comps, lanes)
        base += count

    cos_all, sin_all = jnp.cos(phase[...]), jnp.sin(phase[...])
    cos = [jnp.broadcast_to(cos_all[k : k + 1], (comps, lanes)) for k in range(4)]
    sin = [jnp.broadcast_to(sin_all[k : k + 1], (comps, lanes)) for k in range(4)]

    def aggregate(r, carry):
        first = 0
        for width in widths:
            for c in range(width):
                total_c = total_s = None
                for k in range(4):
                    at = 4 * first + (2 * r + k // 2) * (2 * width) + 2 * c + k % 2
                    piece = spread[at]
                    add_c, add_s = cos[k] * piece, sin[k] * piece
                    total_c = add_c if k == 0 else total_c + add_c
                    total_s = add_s if k == 0 else total_s + add_s
                whole = total_c + times_i(total_s)
                pattern[first + r * width + c] = whole.astype(bf16).astype(f32)
            first += height * width
        return carry

    lax.fori_loop(0, height, aggregate, 0)

    def translate(members, ops_ref, op_of, source, src_of, lane_at):
        cuts = pl.ds(lane_at, HALF)
        sums = [[None, None] for _ in members]
        for t in range(slots):
            op_id = op_of(t)
            real = jnp.broadcast_to(ops_ref[op_id, 0:1, cuts], (comps, HALF))
            imag = jnp.broadcast_to(ops_ref[op_id, 1:2, cuts], (comps, HALF))
            for m, box in enumerate(members):
                piece = source[src_of(box, t), :, cuts]
                add_c, add_s = real * piece, imag * piece
                sums[m][0] = add_c if t == 0 else sums[m][0] + add_c
                sums[m][1] = add_s if t == 0 else sums[m][1] + add_s
        return [a + times_i(b) for a, b in sums]

    for lane_at in range(0, lanes, HALF):
        part = slice(lane_at, lane_at + HALF)
        for c in range(cols):
            for start in range(2):
                group = [r * cols + c for r in range(start, rows, 2)]
                sums = translate(
                    group, pops, lambda t: pop[group[0], t], pattern,
                    lambda box, t: psrc[box, t], lane_at,
                )
                for box, total in zip(group, sums):
                    r = box // cols
                    total = total.astype(bf16).astype(f32)
                    turned = times_i(total)
                    for k in range(4):
                        at = (2 * r + k // 2) * fcols + 2 * c + k % 2
                        value = cos[k][:, part] * total - sin[k][:, part] * turned
                        child[at, :, part] = value.astype(bf16)

    back = lax.dot_general(
        child[...].reshape(frows * fcols * comps, lanes), interp[...],
        (((1,), (1,)), ((), ())), preferred_element_type=f32,
    ).reshape(frows * fcols, comps, fdirs)

    @pl.when(step == 0)
    def _():
        acc[...] = back

    @pl.when(step > 0)
    def _():
        acc[...] += back

    steps = pl.num_programs(0)
    first_box = lax.rem(step, 4) // 2 * fcols + lax.rem(step, 2)

    @pl.when(step < 4)
    def _():
        group = [first_box + 2 * r * fcols + 2 * c for r in range(rows) for c in range(cols)]
        for lane_at in range(0, fdirs, HALF):
            sums = translate(
                group, fops, lambda t: fop[first_box, t], fine, lambda box, t: fsrc[box, t], lane_at
            )
            for box, total in zip(group, sums):
                near[box, :, lane_at : lane_at + HALF] = total

    @pl.when(step == steps - 1)
    def _():
        scale = fdirs / (lanes * steps)
        for r in range(frows):
            for c in range(fcols):
                at = r * fcols + c
                value = near[at] + acc[at] * scale
                out[r, c, 0] = value[:sides]
                out[r, c, 1] = value[sides:]


def per_device(
    fine_out, interp, child_phase, fine_ops, parent_ops, fine_src, fine_op, parent_src, parent_op
):
    frows, fcols, _, sides, fdirs = fine_out.shape
    rows, cols = frows // 2, fcols // 2
    comps = 2 * sides
    pdirs = interp.shape[1]
    patch_odd = lax.rem(lax.axis_index("patch"), 2)
    dir_at = lax.axis_index("dir")
    boxes, fine_tab, fine_ids, par_tab, par_ids = build_tables(rows, cols)

    own = fine_out.reshape(frows * fcols * comps, fdirs)
    patch_halo = exchange(own, "patch", 2 * fcols * comps, rows)
    strip = jnp.concatenate([own] + patch_halo, axis=0)
    assert all(size == cols for size in halo_sizes(cols))
    side_a, side_b = exchange(strip, "dir", 1, cols)

    pops = gather_ops(parent_ops, "dir")

    which = patch_odd * 2 + lax.rem(dir_at, 2)

    def lists(opcode, width, ids, table, none):
        mine = lax.dynamic_slice_in_dim(opcode, dir_at * width, width, 1)
        mine = mine.reshape(-1, 1, mine.shape[2])
        present = jnp.any(mine == ids[:, :, None], axis=2)
        return jnp.where(present, table, none)

    ids_par = jnp.asarray(par_ids)[which]
    fsrc = lists(fine_op, fcols, jnp.asarray(fine_ids), jnp.asarray(fine_tab)[which], 4 * boxes)
    psrc = lists(parent_op, cols, ids_par, jnp.asarray(par_tab)[which], boxes)

    steps = pdirs // CHUNK
    assert steps >= 4 and pdirs % CHUNK == 0 and fdirs % HALF == 0
    smem = pl.BlockSpec(memory_space=pltpu.SMEM)
    vmem = pl.BlockSpec(memory_space=pltpu.VMEM)
    return pl.pallas_call(
        functools.partial(kernel, rows, cols, sides, boxes),
        grid=(steps,),
        out_shape=jax.ShapeDtypeStruct(fine_out.shape, jnp.float32),
        in_specs=[
            smem, smem, smem, smem, vmem, vmem, vmem,
            pl.BlockSpec((fdirs, CHUNK), lambda j: (0, j)),
            pl.BlockSpec((4, CHUNK), lambda j: (0, j)),
            vmem,
            pl.BlockSpec((parent_ops.shape[0], 2, CHUNK), lambda j: (0, 0, j)),
        ],
        out_specs=pl.BlockSpec(fine_out.shape, lambda j: (0,) * 5),
        scratch_shapes=[
            pltpu.VMEM((4 * boxes, comps, CHUNK), jnp.float32),
            pltpu.VMEM((boxes + 1, comps, CHUNK), jnp.float32),
            pltpu.VMEM((4 * boxes + 1, comps, fdirs), jnp.float32),
            pltpu.VMEM((frows * fcols, comps, CHUNK), jnp.bfloat16),
            pltpu.VMEM((frows * fcols, comps, fdirs), jnp.float32),
            pltpu.VMEM((frows * fcols, comps, fdirs), jnp.float32),
        ],
        compiler_params=pltpu.CompilerParams(vmem_limit_bytes=40 * 1024 * 1024),
    )(fsrc, jnp.asarray(fine_ids), psrc, ids_par, strip, side_a, side_b,
      interp, child_phase, fine_ops, pops)


def solution(mesh):
    in_specs = (
        P("patch", "dir", None, None, None),
        P(),
        P(),
        P(),
        P(None, None, "dir"),
        P("patch", None, None),
        P("patch", None, None),
        P("patch", None, None),
        P("patch", None, None),
    )
    out_specs = P("patch", "dir", None, None, None)
    return jax.shard_map(
        per_device, mesh=mesh, in_specs=in_specs, out_specs=out_specs, check_vma=False
    )
```

```python
import functools

import jax
import jax.numpy as jnp
import numpy as np
from jax import lax
from jax.experimental import pallas as pl
from jax.experimental.pallas import tpu as pltpu
from jax.sharding import PartitionSpec as P

CHUNK = 512
F32, BF16 = jnp.float32, jnp.bfloat16


def offset_pairs():
    return [(dr, dc) for dr in range(-3, 4) for dc in range(-3, 4) if max(abs(dr), abs(dc)) > 1]


def class_offsets(row_odd, col_odd):
    return [
        (op_id, dr, dc)
        for op_id, (dr, dc) in enumerate(offset_pairs())
        if -2 <= dr + row_odd <= 3 and -2 <= dc + col_odd <= 3
    ]


def halo_sizes(count):
    return (3, 2) if count % 2 else (2, 2)


def stored_at(rel, count, odd):
    first, second = halo_sizes(count)
    if 0 <= rel < count:
        return rel
    if rel < 0:
        return count + first + rel if odd else count + first + second + rel
    return rel if not odd else rel + first


def place(row, col, rows, cols, row_odd, col_odd, scale):
    at_r = stored_at(row // scale, rows, row_odd) * scale + row % scale
    at_c = stored_at(col // scale, cols, col_odd) * scale + col % scale
    for group, width in enumerate((cols, *halo_sizes(cols))):
        if at_c < width * scale:
            return group, at_r * width * scale + at_c
        at_c -= width * scale


def slots_of(row, col, rows, cols, row_odd, col_odd, scale):
    shift_r, shift_c = (row_odd * rows, col_odd * cols) if scale == 1 else (0, 0)
    found = ([], [], [])
    for op_id, dr, dc in class_offsets((row + shift_r) % 2, (col + shift_c) % 2):
        group, index = place(row + dr, col + dc, rows, cols, row_odd, col_odd, scale)
        found[group].append((op_id, index))
    return found


def slot_counts(rows, cols, scale):
    most = [0, 0, 0]
    for row_odd in range(2):
        for col_odd in range(2):
            for r in range(rows * scale):
                for c in range(cols * scale):
                    lists = slots_of(r, c, rows, cols, row_odd, col_odd, scale)
                    most = [max(m, len(found)) for m, found in zip(most, lists)]
    return most[0], max(most[1:])


def build_tables(rows, cols, zeros):
    fine_own, fine_side = slot_counts(rows, cols, 2)
    par_own, par_side = slot_counts(rows, cols, 1)
    width = max(fine_own + 2 * fine_side, par_own + 2 * par_side)
    sources, op_ids = [], []
    for row_odd in range(2):
        for col_odd in range(2):
            src_rows, id_rows = [], []
            for scale, sizes in ((2, (fine_own, fine_side, fine_side)), (1, (par_own, par_side, par_side))):
                zero = zeros[scale]
                for r in range(rows * scale):
                    for c in range(cols * scale):
                        src_row, id_row = [], []
                        lists = slots_of(r, c, rows, cols, row_odd, col_odd, scale)
                        for size, found in zip(sizes, lists):
                            found = found + [(0, zero)] * (size - len(found))
                            src_row += [s for _, s in found]
                            id_row += [o for o, _ in found]
                        pad = width - len(src_row)
                        src_rows.append(src_row + [zero] * pad)
                        id_rows.append(id_row + [0] * pad)
            sources.append(src_rows)
            op_ids.append(id_rows)
    return np.array(sources, np.int32), np.array(op_ids, np.int32)


def pairs(count, first):
    if first:
        return [(i, i ^ 1) for i in range(count) if (i ^ 1) < count]
    found = []
    for i in range(1, count - 1, 2):
        found += [(i, i + 1), (i + 1, i)]
    return found


def exchange(block, axis, unit, count):
    n = lax.axis_size(axis)
    odd = lax.rem(lax.axis_index(axis), 2)
    got = []
    for first, size in zip((True, False), halo_sizes(count)):
        edge = block
        if size < count:
            low = (1 - odd) if first else odd
            edge = lax.dynamic_slice_in_dim(block, low * ((count - size) * unit), size * unit, 0)
        got.append(lax.ppermute(edge, axis, pairs(n, first)))
    return got


def swap_bits(axis):
    return lax.axis_size(axis).bit_length() - 1


def gather_stage(block, axis, bit):
    other = lax.ppermute(block, axis, [(i, i ^ (1 << bit)) for i in range(lax.axis_size(axis))])
    return jnp.concatenate([block, other], axis=0)


def in_order(block, axis):
    n, bits = lax.axis_size(axis), swap_bits(axis)
    spots = [int(format(s, "0%db" % bits)[::-1], 2) for s in range(n)] if bits else [0]
    at = jnp.asarray(np.array(spots, np.int32))[jnp.arange(n, dtype=jnp.int32) ^ lax.axis_index(axis)]
    block = jnp.take(block, at, axis=0)
    return block.transpose(1, 2, 0, 3).reshape(1, block.shape[1], 2, n * block.shape[3])


def times_i(v, sides):
    sign = jnp.where(lax.broadcasted_iota(jnp.int32, (2 * sides, 1), 0) < sides, -1.0, 1.0)
    return sign.astype(F32) * pltpu.roll(v, sides, 0)


def row_of(ref, lead, part, lane, width, comps):
    return jnp.broadcast_to(ref[(*lead, slice(part, part + 1), pl.ds(lane, width))], (comps, width))


def add_slots(sums, coefs, pieces):
    real, imag = coefs
    for m, piece in enumerate(pieces):
        add = [real * piece, imag * piece]
        sums[m] = add if sums[m] is None else [a + b for a, b in zip(sums[m], add)]


def widen(src, fine, comps):
    count = src.shape[0] // comps
    fine[:count] = src[...].astype(F32).reshape(count, comps, src.shape[1])
    fine[count] = jnp.zeros(fine.shape[1:], F32)


def spread_chunk(src, interp, j, buffer, comps):
    lanes = slice(j * CHUNK, (j + 1) * CHUNK)
    out = jnp.dot(src[...], interp[:, lanes], preferred_element_type=F32)
    buffer[...] = out.reshape(-1, comps, CHUNK)


def shifts(trig, j, comps):
    lanes = slice(j * CHUNK, (j + 1) * CHUNK)
    return [jnp.broadcast_to(trig[k : k + 1, lanes], (comps, CHUNK)) for k in range(8)]


def aggregate_chunk(buffer, shift, pattern, lanes, width, sides):
    boxes = buffer.shape[0] // 4
    for q in range(boxes):
        r, c = divmod(q, width)
        total = [None, None]
        for k in range(4):
            piece = buffer[(2 * r + k // 2) * (2 * width) + 2 * c + k % 2]
            for i in range(2):
                add = shift[4 * i + k] * piece
                total[i] = add if k == 0 else total[i] + add
        whole = total[0] + times_i(total[1], sides)
        pattern[q, :, lanes] = whole.astype(BF16).astype(F32)
    pattern[boxes, :, lanes] = jnp.zeros(whole.shape, F32)


def near_side(table, ids, fops, fine, rows, cols, sides, base, count, first_col, store):
    comps, fdirs = fine.shape[1:]
    for a in range(2):
        for c in range(2):
            group = [(2 * r + a) * (2 * cols) + first_col + c for r in range(rows)]
            sums = [None] * rows
            for t in range(base, base + count):
                op_id = ids[group[0], t]
                coefs = [row_of(fops, (op_id,), i, 0, fdirs, comps) for i in range(2)]
                add_slots(sums, coefs, [fine[table[box, t]] for box in group])
            for r in range(rows):
                store((2 * r + a) * 2 + c, sums[r][0] + times_i(sums[r][1], sides))


def own_kernel(rows, cols, sides, table, src, interp, phase, fops, pattern, near, trig, fine, even, odd):
    comps, fdirs = fine.shape[1:]
    buffers = (even, odd)
    steps = interp.shape[1] // CHUNK
    trig[:4] = jnp.cos(phase[...])
    trig[4:] = jnp.sin(phase[...])
    widen(src, fine, comps)
    spread_chunk(src, interp, 0, buffers[0], comps)
    for j in range(steps):
        if j + 1 < steps:
            spread_chunk(src, interp, j + 1, buffers[(j + 1) % 2], comps)
        lanes = slice(j * CHUNK, (j + 1) * CHUNK)
        aggregate_chunk(buffers[j % 2], shifts(trig, j, comps), pattern, lanes, cols, sides)
    for a in range(2):
        for c in range(2 * cols):
            found = slots_of(a, c, rows, cols, 0, 0, 2)[0]
            group = [(2 * r + a) * (2 * cols) + c for r in range(rows)]
            sums = [None] * rows
            for t, (op_id, _) in enumerate(found):
                coefs = [row_of(fops, (op_id,), i, 0, fdirs, comps) for i in range(2)]
                add_slots(sums, coefs, [fine[table[box, t]] for box in group])
            for box, (real, imag) in zip(group, sums):
                near[box] = real + times_i(imag, sides)


def side_kernel(rows, cols, sides, table, ids, info, src, interp, trig, fops, pattern, near, fine, even, odd):
    comps = fine.shape[1]
    buffers = (even, odd)
    steps = interp.shape[1] // CHUNK
    own, side = slot_counts(rows, cols, 2)
    width = halo_sizes(cols)[0]
    widen(src, fine, comps)

    def store(at, value):
        near[at] = value

    spread_chunk(src, interp, 0, buffers[0], comps)
    for j in range(steps):
        if j + 1 < steps:
            spread_chunk(src, interp, j + 1, buffers[(j + 1) % 2], comps)
        lanes = slice(j * CHUNK, (j + 1) * CHUNK)
        aggregate_chunk(buffers[j % 2], shifts(trig, j, comps), pattern, lanes, width, sides)
    near_side(table, ids, fops, fine, rows, cols, sides, own, side, info[0, 0] * (2 * cols - 2), store)


def last_kernel(
    rows, cols, sides,
    table, ids, info,
    src, interp, trig, fops, pops, pat_own, pat_a, near_own, near_a,
    out,
    fine, even, odd, pat_b0, pat_b1, child0, child1, near_b, acc,
):
    comps, fdirs = fine.shape[1:]
    fcols = 2 * cols
    width = halo_sizes(cols)[1]
    steps = interp.shape[1] // CHUNK
    buffers, patterns, children = (even, odd), (pat_b0, pat_b1), (child0, child1)
    own, side = slot_counts(rows, cols, 2)
    par_own, par_side = slot_counts(rows, cols, 1)
    a_right = info[0, 0]
    piece_w = min(CHUNK, pops.shape[3])

    widen(src, fine, comps)

    def store(at, value):
        near_b[1 - a_right, at] = value

    spread_chunk(src, interp, 0, buffers[0], comps)
    near_side(
        table, ids, fops, fine, rows, cols, sides, own + side, side, (1 - a_right) * (fcols - 2), store
    )
    for at in range(near_a.shape[0]):
        near_b[a_right, at] = near_a[at]

    for j in range(steps):
        if j + 1 < steps:
            spread_chunk(src, interp, j + 1, buffers[(j + 1) % 2], comps)
        shift = shifts(trig, j, comps)
        lanes = slice(j * CHUNK, (j + 1) * CHUNK)
        pat_b, child = patterns[j % 2], children[j % 2]
        aggregate_chunk(buffers[j % 2], shift, pat_b, slice(0, CHUNK), width, sides)
        spots = []
        for lane in range(j * CHUNK, (j + 1) * CHUNK, piece_w):
            spots.append((info[1, lane // pops.shape[3]], lane % pops.shape[3]))
        for c in range(cols):
            for start in range(2):
                members = range(start, rows, 2)
                group = [2 * rows * fcols + r * cols + c for r in members]
                sums = [None] * len(group)
                for first, count, ref, cut in (
                    (0, par_own, pat_own, lanes),
                    (par_own, par_side, pat_a, lanes),
                    (par_own + par_side, par_side, pat_b, slice(0, CHUNK)),
                ):
                    for t in range(first, first + count):
                        op_id = ids[group[0], t]
                        coefs = [
                            jnp.concatenate(
                                [row_of(pops, (e, op_id), i, at, piece_w, comps) for e, at in spots], axis=1
                            )
                            for i in range(2)
                        ]
                        add_slots(sums, coefs, [ref[table[box, t], :, cut] for box in group])
                for r, (real, imag) in zip(members, sums):
                    total = (real + times_i(imag, sides)).astype(BF16).astype(F32)
                    turned = times_i(total, sides)
                    for k in range(4):
                        at = (2 * r + k // 2) * fcols + 2 * c + k % 2
                        child[at] = (shift[k] * total - shift[4 + k] * turned).astype(BF16)
        back = lax.dot_general(
            child[...].reshape(-1, CHUNK), interp[:, lanes], (((1,), (1,)), ((), ())),
            preferred_element_type=F32,
        ).reshape(acc.shape)
        acc[...] = back if j == 0 else acc[...] + back

    scale = fdirs / interp.shape[1]
    for r in range(2 * rows):
        for c in range(fcols):
            at = r * fcols + c
            value = near_own[at] + acc[at] * scale
            if c < 2:
                value = value + near_b[0, r * 2 + c]
            if c >= fcols - 2:
                value = value + near_b[1, r * 2 + c - (fcols - 2)]
            out[r, c, 0] = value[:sides]
            out[r, c, 1] = value[sides:]


def per_device(
    fine_out, interp, child_phase, fine_ops, parent_ops, fine_src, fine_op, parent_src, parent_op
):
    frows, fcols, _, sides, fdirs = fine_out.shape
    rows, cols = frows // 2, fcols // 2
    comps = 2 * sides
    pdirs = interp.shape[1]
    assert all(size == cols for size in halo_sizes(cols)) and pdirs % CHUNK == 0
    patch_odd = lax.rem(lax.axis_index("patch"), 2)
    dir_at = lax.axis_index("dir")
    dir_odd = lax.rem(dir_at, 2)
    height = rows + sum(halo_sizes(rows))
    boxes = height * cols
    n_dir, bits = lax.axis_size("dir"), swap_bits("dir")

    own = fine_out.reshape(frows * fcols * comps, fdirs)
    patch_halo = exchange(own, "patch", 2 * fcols * comps, rows)
    strip = jnp.concatenate([own] + patch_halo, axis=0)
    side_a, side_b = exchange(strip, "dir", 1, cols)

    pops = parent_ops[None]
    for bit in reversed(range(bits)):
        pops = gather_stage(pops, "dir", bit)
    shard = parent_ops.shape[2]
    if shard % 128 == 0 and CHUNK % shard == 0:
        spots = functools.reduce(
            jnp.add, [(((jnp.arange(n_dir, dtype=jnp.int32) ^ dir_at) >> b) & 1) << (bits - 1 - b) for b in range(bits)],
            jnp.zeros((n_dir,), jnp.int32),
        )
    else:
        pops = in_order(pops, "dir")
        spots = jnp.zeros((n_dir,), jnp.int32)
    info = jnp.stack([jnp.full((n_dir,), 1 - dir_odd, jnp.int32), spots])

    sources, op_ids = build_tables(rows, cols, {2: 4 * boxes, 1: boxes})
    which = patch_odd * 2 + dir_odd
    sources, ids = jnp.asarray(sources)[which], jnp.asarray(op_ids)[which]
    lists = jnp.concatenate([
        lax.dynamic_slice_in_dim(op, dir_at * width, width, 1).reshape(-1, 1, op.shape[2])
        for op, width in ((fine_op, fcols), (parent_op, cols))
    ])
    present = jnp.any(lists == ids[:, :, None], axis=2)
    nothing = np.array([4 * boxes] * (frows * fcols) + [boxes] * (rows * cols), np.int32)[:, None]
    table = jnp.where(present, sources, jnp.asarray(nothing))

    smem = pl.BlockSpec(memory_space=pltpu.SMEM)
    vmem = pl.BlockSpec(memory_space=pltpu.VMEM)
    params = pltpu.CompilerParams(vmem_limit_bytes=40 * 1024 * 1024)
    pattern = jax.ShapeDtypeStruct((boxes + 1, comps, pdirs), F32)
    fine_scratch = pltpu.VMEM((4 * boxes + 1, comps, fdirs), F32)
    spread = pltpu.VMEM((4 * boxes, comps, CHUNK), F32)
    half_pattern = pltpu.VMEM((boxes + 1, comps, CHUNK), F32)
    child = pltpu.VMEM((frows * fcols, comps, CHUNK), BF16)
    pat_own, near_own, trig = pl.pallas_call(
        functools.partial(own_kernel, rows, cols, sides),
        out_shape=[
            pattern,
            jax.ShapeDtypeStruct((frows * fcols, comps, fdirs), F32),
            jax.ShapeDtypeStruct((8, pdirs), F32),
        ],
        in_specs=[smem] + [vmem] * 4,
        out_specs=[vmem] * 3,
        scratch_shapes=[fine_scratch, spread, spread],
        compiler_params=params,
        name="own",
    )(table, strip, interp, child_phase, fine_ops)
    pat_a, near_a = pl.pallas_call(
        functools.partial(side_kernel, rows, cols, sides),
        out_shape=[pattern, jax.ShapeDtypeStruct((frows * 2, comps, fdirs), F32)],
        in_specs=[smem] * 3 + [vmem] * 4,
        out_specs=[vmem] * 2,
        scratch_shapes=[fine_scratch, spread, spread],
        compiler_params=params,
        name="side",
    )(table, ids, info, side_a, interp, trig, fine_ops)
    return pl.pallas_call(
        functools.partial(last_kernel, rows, cols, sides),
        out_shape=jax.ShapeDtypeStruct(fine_out.shape, F32),
        in_specs=[smem] * 3 + [vmem] * 9,
        out_specs=vmem,
        scratch_shapes=[
            fine_scratch, spread, spread, half_pattern, half_pattern, child, child,
            pltpu.VMEM((2, frows * 2, comps, fdirs), F32),
            pltpu.VMEM((frows * fcols, comps, fdirs), F32),
        ],
        compiler_params=params,
        name="last",
    )(table, ids, info, side_b, interp, trig, fine_ops, pops, pat_own, pat_a, near_own, near_a)


def solution(mesh):
    in_specs = (
        P("patch", "dir", None, None, None),
        P(),
        P(),
        P(),
        P(None, None, "dir"),
        P("patch", None, None),
        P("patch", None, None),
        P("patch", None, None),
        P("patch", None, None),
    )
    out_specs = P("patch", "dir", None, None, None)
    return jax.shard_map(
        per_device, mesh=mesh, in_specs=in_specs, out_specs=out_specs, check_vma=False
    )
```

```python
import functools

import jax
import jax.numpy as jnp
import numpy as np
from jax import lax
from jax.experimental import pallas as pl
from jax.experimental.pallas import tpu as pltpu
from jax.sharding import PartitionSpec as P

CHUNK = 512
F32, BF16 = jnp.float32, jnp.bfloat16


def offset_pairs():
    return [(dr, dc) for dr in range(-3, 4) for dc in range(-3, 4) if max(abs(dr), abs(dc)) > 1]


def class_offsets(row_odd, col_odd):
    return [
        (op_id, dr, dc)
        for op_id, (dr, dc) in enumerate(offset_pairs())
        if -2 <= dr + row_odd <= 3 and -2 <= dc + col_odd <= 3
    ]


def halo_sizes(count):
    return (3, 2) if count % 2 else (2, 2)


def stored_at(rel, count, odd):
    first, second = halo_sizes(count)
    if 0 <= rel < count:
        return rel
    if rel < 0:
        return count + first + rel if odd else count + first + second + rel
    return rel if not odd else rel + first


def place(row, col, rows, cols, row_odd, col_odd, scale):
    at_r = stored_at(row // scale, rows, row_odd) * scale + row % scale
    at_c = stored_at(col // scale, cols, col_odd) * scale + col % scale
    for group, width in enumerate((cols, *halo_sizes(cols))):
        if at_c < width * scale:
            return group, at_r * width * scale + at_c
        at_c -= width * scale


def fine_slots(row, col, rows, cols, row_odd, col_odd):
    inside, found = 4 * rows * cols, ([], [], [], [])
    for op_id, dr, dc in class_offsets(row % 2, col % 2):
        group, index = place(row + dr, col + dc, rows, cols, row_odd, col_odd, 2)
        if group:
            found[group + 1].append((op_id, index))
        elif index >= inside:
            found[0].append((op_id, None))
            found[1].append((op_id, index - inside))
        else:
            found[0].append((op_id, index))
    return found


def parent_slots(row, col, rows, cols, row_odd, col_odd):
    found = ([], [], [])
    for op_id, dr, dc in class_offsets((row + row_odd * rows) % 2, (col + col_odd * cols) % 2):
        group, index = place(row + dr, col + dc, rows, cols, row_odd, col_odd, 1)
        found[group].append((op_id, index))
    return found


PARITIES = [(a, b) for a in range(2) for b in range(2)]


def slot_counts(rows, cols, scale):
    slots = fine_slots if scale == 2 else parent_slots
    lists = [
        [len(found) for found in slots(r, c, rows, cols, *odd)]
        for odd in PARITIES for r in range(rows * scale) for c in range(cols * scale)
    ]
    most = [max(column) for column in zip(*lists)]
    return most[:-2] + [max(most[-2:])] * 2


def starts(counts):
    return [sum(counts[:i]) for i in range(len(counts))]


def build_tables(rows, cols, zeros):
    counts = {scale: slot_counts(rows, cols, scale) for scale in (2, 1)}
    width = max(sum(c) for c in counts.values())
    sources, op_ids, nothing = [], [], []
    for odd in PARITIES:
        src_rows, id_rows, none_rows = [], [], []
        for scale, slots in ((2, fine_slots), (1, parent_slots)):
            for r in range(rows * scale):
                for c in range(cols * scale):
                    src_row, id_row, none_row = [], [], []
                    for size, found, zero in zip(counts[scale], slots(r, c, rows, cols, *odd), zeros[scale]):
                        found = found + [(0, None)] * (size - len(found))
                        src_row += [zero if at is None else at for _, at in found]
                        id_row += [o for o, _ in found]
                        none_row += [zero] * size
                    pad = [0] * (width - len(src_row))
                    src_rows.append(src_row + pad)
                    id_rows.append(id_row + pad)
                    none_rows.append(none_row + pad)
        sources.append(src_rows)
        op_ids.append(id_rows)
        nothing = none_rows
    return np.array(sources, np.int32), np.array(op_ids, np.int32), np.array(nothing, np.int32)


def pairs(count, first):
    if first:
        return [(i, i ^ 1) for i in range(count) if (i ^ 1) < count]
    found = []
    for i in range(1, count - 1, 2):
        found += [(i, i + 1), (i + 1, i)]
    return found


def exchange(block, axis, unit, count):
    n = lax.axis_size(axis)
    odd = lax.rem(lax.axis_index(axis), 2)
    got = []
    for first, size in zip((True, False), halo_sizes(count)):
        edge = block
        if size < count:
            low = (1 - odd) if first else odd
            edge = lax.dynamic_slice_in_dim(block, low * ((count - size) * unit), size * unit, 0)
        got.append(lax.ppermute(edge, axis, pairs(n, first)))
    return got


def swap_bits(axis):
    return lax.axis_size(axis).bit_length() - 1


def in_order(block, axis):
    n, bits = lax.axis_size(axis), swap_bits(axis)
    spots = [int(format(s, "0%db" % bits)[::-1], 2) for s in range(n)] if bits else [0]
    at = jnp.asarray(np.array(spots, np.int32))[jnp.arange(n, dtype=jnp.int32) ^ lax.axis_index(axis)]
    block = jnp.take(block, at, axis=0)
    return block.transpose(1, 2, 0, 3).reshape(1, block.shape[1], 2, n * block.shape[3])


def times_i(v, sides):
    sign = jnp.where(lax.broadcasted_iota(jnp.int32, (2 * sides, 1), 0) < sides, -1.0, 1.0)
    return sign.astype(F32) * pltpu.roll(v, sides, 0)


def row_of(ref, lead, part, lane, width, comps):
    return jnp.broadcast_to(ref[(*lead, slice(part, part + 1), pl.ds(lane, width))], (comps, width))


def add_slots(sums, coefs, pieces):
    real, imag = coefs
    for m, piece in enumerate(pieces):
        add = [real * piece, imag * piece]
        sums[m] = add if sums[m] is None else [a + b for a, b in zip(sums[m], add)]


def widen(src, fine, comps):
    count = src.shape[0] // comps
    fine[:count] = src[...].astype(F32).reshape(count, comps, src.shape[1])
    fine[count] = jnp.zeros(fine.shape[1:], F32)


def spread_chunk(src, interp, j, buffer, comps):
    lanes = slice(j * CHUNK, (j + 1) * CHUNK)
    out = jnp.dot(src[...], interp[:, lanes], preferred_element_type=F32)
    buffer[...] = out.reshape(-1, comps, CHUNK)


def shifts(trig, j, comps, width=CHUNK):
    lanes = slice(j * CHUNK, j * CHUNK + width)
    return [jnp.broadcast_to(trig[k : k + 1, lanes], (comps, width)) for k in range(8)]


def aggregate_chunk(buffer, shift, pattern, lanes, width, sides, base=0):
    for q in range(buffer.shape[0] // 4):
        r, c = divmod(q, width)
        total = [None, None]
        for k in range(4):
            piece = buffer[(2 * r + k // 2) * (2 * width) + 2 * c + k % 2]
            for i in range(2):
                add = shift[4 * i + k] * piece
                total[i] = add if k == 0 else total[i] + add
        whole = total[0] + times_i(total[1], sides)
        pattern[base + q, :, lanes] = whole.astype(BF16).astype(F32)


def aggregate(src, interp, trig, buffers, pattern, width, sides, base=0, done=lambda j: None):
    comps = 2 * sides
    steps = interp.shape[1] // CHUNK
    spread_chunk(src, interp, 0, buffers[0], comps)
    for j in range(steps):
        if j + 1 < steps:
            spread_chunk(src, interp, j + 1, buffers[(j + 1) % 2], comps)
        lanes = slice(j * CHUNK, (j + 1) * CHUNK)
        aggregate_chunk(buffers[j % 2], shifts(trig, j, comps), pattern, lanes, width, sides, base)
        done(j)


def zero_box(pattern):
    pattern[pattern.shape[0] - 1] = jnp.zeros(pattern.shape[1:], F32)


def near_sums(table, fops, fine, group, base, op_ids):
    comps, fdirs = fine.shape[1:]
    sums = [None] * len(group)
    for t, op_id in enumerate(op_ids, base):
        coefs = [row_of(fops, (op_id,), i, 0, fdirs, comps) for i in range(2)]
        add_slots(sums, coefs, [fine[table[box, t]] for box in group])
    return [real + times_i(imag, comps // 2) for real, imag in sums]


def near_side(table, ids, fops, fine, rows, cols, base, count, first_col, store):
    for a in range(2):
        for c in range(2):
            group = [(2 * r + a) * (2 * cols) + first_col + c for r in range(rows)]
            op_ids = [ids[group[0], t] for t in range(base, base + count)]
            for r, value in enumerate(near_sums(table, fops, fine, group, base, op_ids)):
                store((2 * r + a) * 2 + c, value)


def block_kernel(rows, cols, sides, table, src, interp, phase, fops, pattern, near, trig, fine, even, odd):
    trig[:4] = jnp.cos(phase[...])
    trig[4:] = jnp.sin(phase[...])
    widen(src, fine, 2 * sides)
    aggregate(src, interp, trig, (even, odd), pattern, cols, sides)
    for a in range(2):
        for c in range(2 * cols):
            op_ids = [o for o, _ in fine_slots(a, c, rows, cols, 0, 0)[0]]
            group = [(2 * r + a) * (2 * cols) + c for r in range(rows)]
            for box, value in zip(group, near_sums(table, fops, fine, group, 0, op_ids)):
                near[box] = value


def halo_kernel(
    rows, cols, sides, table, src, interp, trig, fops, pat_block, near_block, pattern, near, fine, even, odd
):
    base = starts(slot_counts(rows, cols, 2))[1]
    widen(src, fine, 2 * sides)
    near[...] = near_block[...]
    pattern[: pat_block.shape[0]] = pat_block[...]
    aggregate(src, interp, trig, (even, odd), pattern, cols, sides, pat_block.shape[0])
    zero_box(pattern)
    for r in range(2 * rows):
        for c in range(2 * cols):
            op_ids = [o for o, _ in fine_slots(r, c, rows, cols, 0, 0)[1]]
            if op_ids:
                box = r * 2 * cols + c
                near[box] += near_sums(table, fops, fine, [box], base, op_ids)[0]


def side_kernel(rows, cols, sides, table, ids, info, src, interp, trig, fops, pattern, near, fine, even, odd):
    counts = slot_counts(rows, cols, 2)
    widen(src, fine, 2 * sides)

    def store(at, value):
        near[at] = value

    aggregate(src, interp, trig, (even, odd), pattern, halo_sizes(cols)[0], sides)
    zero_box(pattern)
    near_side(
        table, ids, fops, fine, rows, cols, starts(counts)[2], counts[2], info[0, 0] * (2 * cols - 2), store
    )


def parent_groups(rows, cols):
    return [[(r, c) for r in range(start, rows, 2)] for c in range(cols) for start in range(2)]


def parent_sums(rows, cols, sides, table, ids, pops, sources, group, first, width):
    comps = 2 * sides
    rows_at = [4 * rows * cols + r * cols + c for r, c in group]
    sums = [None] * len(group)
    for base, count, ref in sources:
        for t in range(base, base + count):
            op_id = ids[rows_at[0], t]
            coefs = [row_of(pops, (op_id,), i, first, width, comps) for i in range(2)]
            add_slots(sums, coefs, [ref[table[row, t], :, first : first + width] for row in rows_at])
    return sums


def inner_kernel(rows, cols, sides, table, ids, info, pat_own, pat_a, *refs):
    *shards, pops, real, imag = refs
    at = 0
    for ref in shards:
        held = ref.shape[3]
        for k in range(ref.shape[0]):
            lane = pl.multiple_of(info[1, at] * held, held)
            pops[:, :, pl.ds(lane, held)] = ref[k]
            at += 1
    counts = slot_counts(rows, cols, 1)
    at = starts(counts)
    sources = [(at[0], counts[0], pat_own), (at[1], counts[1], pat_a)]
    for first in range(0, real.shape[2], 2 * CHUNK):
        for group in parent_groups(rows, cols):
            sums = parent_sums(
                rows, cols, sides, table, ids, pops, sources, group, first, 2 * CHUNK
            )
            for (r, c), (re, im) in zip(group, sums):
                real[r * cols + c, :, first : first + 2 * CHUNK] = re
                imag[r * cols + c, :, first : first + 2 * CHUNK] = im


def last_kernel(
    rows, cols, sides,
    table, ids, info,
    src, interp, trig, fops, pops, real, imag, near_own, near_a,
    out,
    fine, even, odd, pat_b, child, near_b, acc,
):
    comps, fdirs = fine.shape[1:]
    fcols = 2 * cols
    wide = 2 * CHUNK
    counts = slot_counts(rows, cols, 2)
    par_counts = slot_counts(rows, cols, 1)
    a_right = info[0, 0]
    widen(src, fine, comps)
    zero_box(pat_b)

    def store(at, value):
        near_b[1 - a_right, at] = value

    near_side(
        table, ids, fops, fine, rows, cols, starts(counts)[3], counts[3], (1 - a_right) * (fcols - 2), store
    )
    for at in range(near_a.shape[0]):
        near_b[a_right, at] = near_a[at]

    def far(j):
        if j % 2 == 0:
            return
        first = (j - 1) * CHUNK
        shift = shifts(trig, j - 1, comps, wide)
        sources = [(starts(par_counts)[2], par_counts[2], pat_b)]
        for group in parent_groups(rows, cols):
            sums = parent_sums(rows, cols, sides, table, ids, pops, sources, group, first, wide)
            for (r, c), (re, im) in zip(group, sums):
                box = r * cols + c
                re = re + real[box, :, first : first + wide]
                im = im + imag[box, :, first : first + wide]
                total = (re + times_i(im, sides)).astype(BF16).astype(F32)
                turned = times_i(total, sides)
                for k in range(4):
                    at = (2 * r + k // 2) * fcols + 2 * c + k % 2
                    child[at, :, first : first + wide] = (
                        shift[k] * total - shift[4 + k] * turned
                    ).astype(BF16)
        back = lax.dot_general(
            child[:, :, first : first + wide].reshape(-1, wide), interp[:, first : first + wide],
            (((1,), (1,)), ((), ())), preferred_element_type=F32,
        ).reshape(acc.shape)
        acc[...] = back if j == 1 else acc[...] + back

    aggregate(src, interp, trig, (even, odd), pat_b, halo_sizes(cols)[1], sides, 0, far)

    scale = fdirs / interp.shape[1]
    for r in range(2 * rows):
        for c in range(fcols):
            at = r * fcols + c
            value = near_own[at] + acc[at] * scale
            if c < 2:
                value = value + near_b[0, r * 2 + c]
            if c >= fcols - 2:
                value = value + near_b[1, r * 2 + c - (fcols - 2)]
            out[r, c, 0] = value[:sides]
            out[r, c, 1] = value[sides:]


def per_device(
    fine_out, interp, child_phase, fine_ops, parent_ops, fine_src, fine_op, parent_src, parent_op
):
    frows, fcols, _, sides, fdirs = fine_out.shape
    rows, cols = frows // 2, fcols // 2
    comps = 2 * sides
    pdirs = interp.shape[1]
    assert all(size == cols for size in halo_sizes(cols)) and pdirs % (2 * CHUNK) == 0
    patch_odd = lax.rem(lax.axis_index("patch"), 2)
    dir_at = lax.axis_index("dir")
    dir_odd = lax.rem(dir_at, 2)
    height = rows + sum(halo_sizes(rows))
    boxes = height * cols
    n_dir, bits = lax.axis_size("dir"), swap_bits("dir")

    own = fine_out.reshape(frows * fcols * comps, fdirs)
    patch_halo = exchange(own, "patch", 2 * fcols * comps, rows)
    strip = jnp.concatenate([own] + patch_halo, axis=0)
    side_a, side_b = exchange(strip, "dir", 1, cols)

    shards = [parent_ops[None]]
    for bit in reversed(range(bits)):
        held = jnp.concatenate(shards, axis=0)
        shards.append(lax.ppermute(held, "dir", [(i, i ^ (1 << bit)) for i in range(n_dir)]))
    if parent_ops.shape[2] % 128 == 0:
        places = jnp.arange(n_dir, dtype=jnp.int32)
        spots = dir_at
        for b in range(bits):
            spots = spots ^ (((places >> b) & 1) << (bits - 1 - b))
    else:
        shards = [in_order(jnp.concatenate(shards, axis=0), "dir")]
        spots = jnp.zeros((n_dir,), jnp.int32)
    info = jnp.stack([jnp.full((n_dir,), 1 - dir_odd, jnp.int32), spots])

    outside = boxes - rows * cols
    sources, op_ids, nothing = build_tables(
        rows, cols, {2: [frows * fcols, 4 * outside, 4 * boxes, 4 * boxes], 1: [boxes] * 3}
    )
    which = patch_odd * 2 + dir_odd
    sources, ids = jnp.asarray(sources)[which], jnp.asarray(op_ids)[which]
    lists = jnp.concatenate([
        lax.dynamic_slice_in_dim(op, dir_at * width, width, 1).reshape(-1, 1, op.shape[2])
        for op, width in ((fine_op, fcols), (parent_op, cols))
    ])
    present = jnp.any(lists == ids[:, :, None], axis=2)
    table = jnp.where(present, sources, jnp.asarray(nothing))

    smem = pl.BlockSpec(memory_space=pltpu.SMEM)
    vmem = pl.BlockSpec(memory_space=pltpu.VMEM)

    def shape(*dims):
        return jax.ShapeDtypeStruct(dims, F32)

    def scratch(*dims, kind=F32):
        return pltpu.VMEM(dims, kind)

    def group_scratch(count):
        return [scratch(count + 1, comps, fdirs)] + [scratch(count, comps, CHUNK)] * 2

    def call(body, name, n_smem, outs, scratches, *args):
        return pl.pallas_call(
            functools.partial(body, rows, cols, sides),
            out_shape=outs,
            in_specs=[smem] * n_smem + [vmem] * (len(args) - n_smem),
            out_specs=[vmem] * len(outs),
            scratch_shapes=scratches,
            compiler_params=pltpu.CompilerParams(vmem_limit_bytes=40 * 1024 * 1024),
            name=name,
        )(*args)

    near = shape(frows * fcols, comps, fdirs)
    pattern = shape(boxes + 1, comps, pdirs)
    pat_block, near_block, trig = call(
        block_kernel, "block", 1,
        [shape(rows * cols, comps, pdirs), near, shape(8, pdirs)], group_scratch(frows * fcols),
        table, own, interp, child_phase, fine_ops,
    )
    pat_own, near_own = call(
        halo_kernel, "halo", 1, [pattern, near], group_scratch(4 * outside),
        table, strip[own.shape[0] :], interp, trig, fine_ops, pat_block, near_block,
    )
    pat_a, near_a = call(
        side_kernel, "side", 3, [pattern, shape(frows * 2, comps, fdirs)], group_scratch(4 * boxes),
        table, ids, info, side_a, interp, trig, fine_ops,
    )
    part = shape(rows * cols, comps, pdirs)
    pops, real, imag = call(
        inner_kernel, "inner", 3, [shape(parent_ops.shape[0], 2, pdirs), part, part], [],
        table, ids, info, pat_own, pat_a, *shards,
    )
    return call(
        last_kernel, "last", 3, [jax.ShapeDtypeStruct(fine_out.shape, F32)],
        group_scratch(4 * boxes) + [
            scratch(boxes + 1, comps, pdirs),
            scratch(frows * fcols, comps, pdirs, kind=BF16),
            scratch(2, frows * 2, comps, fdirs),
            scratch(frows * fcols, comps, fdirs),
        ],
        table, ids, info, side_b, interp, trig, fine_ops, pops, real, imag, near_own, near_a,
    )[0]


def solution(mesh):
    in_specs = (
        P("patch", "dir", None, None, None),
        P(),
        P(),
        P(),
        P(None, None, "dir"),
        P("patch", None, None),
        P("patch", None, None),
        P("patch", None, None),
        P("patch", None, None),
    )
    out_specs = P("patch", "dir", None, None, None)
    return jax.shard_map(
        per_device, mesh=mesh, in_specs=in_specs, out_specs=out_specs, check_vma=False
    )
```

```python
import functools

import jax
import jax.numpy as jnp
import numpy as np
from jax import lax
from jax.experimental import pallas as pl
from jax.experimental.pallas import tpu as pltpu
from jax.sharding import PartitionSpec as P

CHUNK = 512
LIMITS = {"block": 8, "pack": 4, "own": 16, "side": 16, "inner": 12, "last": 24}
F32, BF16 = jnp.float32, jnp.bfloat16


def offset_pairs():
    return [(dr, dc) for dr in range(-3, 4) for dc in range(-3, 4) if max(abs(dr), abs(dc)) > 1]


def class_offsets(row_odd, col_odd):
    return [
        (op_id, dr, dc)
        for op_id, (dr, dc) in enumerate(offset_pairs())
        if -2 <= dr + row_odd <= 3 and -2 <= dc + col_odd <= 3
    ]


def halo_sizes(count):
    return (3, 2) if count % 2 else (2, 2)


def stored_at(rel, count, odd):
    first, second = halo_sizes(count)
    if 0 <= rel < count:
        return rel
    if rel < 0:
        return count + first + rel if odd else count + first + second + rel
    return rel if not odd else rel + first


def place(row, col, rows, cols, row_odd, col_odd, scale):
    at_r = stored_at(row // scale, rows, row_odd) * scale + row % scale
    at_c = stored_at(col // scale, cols, col_odd) * scale + col % scale
    for group, width in enumerate((cols, *halo_sizes(cols))):
        if at_c < width * scale:
            return group, at_r * width * scale + at_c
        at_c -= width * scale


def fine_slots(row, col, rows, cols, row_odd, col_odd):
    inside, found = 4 * rows * cols, ([], [], [], [])
    for op_id, dr, dc in class_offsets(row % 2, col % 2):
        group, index = place(row + dr, col + dc, rows, cols, row_odd, col_odd, 2)
        if group:
            found[group + 1].append((op_id, index))
        elif index >= inside:
            found[0].append((op_id, None))
            found[1].append((op_id, index - inside))
        else:
            found[0].append((op_id, index))
    return found


def parent_slots(row, col, rows, cols, row_odd, col_odd):
    found = ([], [], [])
    for op_id, dr, dc in class_offsets((row + row_odd * rows) % 2, (col + col_odd * cols) % 2):
        group, index = place(row + dr, col + dc, rows, cols, row_odd, col_odd, 1)
        found[group].append((op_id, index))
    return found


PARITIES = [(a, b) for a in range(2) for b in range(2)]


def slot_counts(rows, cols, scale):
    slots = fine_slots if scale == 2 else parent_slots
    lists = [
        [len(found) for found in slots(r, c, rows, cols, *odd)]
        for odd in PARITIES for r in range(rows * scale) for c in range(cols * scale)
    ]
    most = [max(column) for column in zip(*lists)]
    return most[:-2] + [max(most[-2:])] * 2


def starts(counts):
    return [sum(counts[:i]) for i in range(len(counts))]


def build_tables(rows, cols, zeros):
    counts = {scale: slot_counts(rows, cols, scale) for scale in (2, 1)}
    width = max(sum(c) for c in counts.values())
    sources, op_ids, nothing = [], [], []
    for odd in PARITIES:
        src_rows, id_rows, none_rows = [], [], []
        for scale, slots in ((2, fine_slots), (1, parent_slots)):
            for r in range(rows * scale):
                for c in range(cols * scale):
                    src_row, id_row, none_row = [], [], []
                    for size, found, zero in zip(counts[scale], slots(r, c, rows, cols, *odd), zeros[scale]):
                        found = found + [(0, None)] * (size - len(found))
                        src_row += [zero if at is None else at for _, at in found]
                        id_row += [o for o, _ in found]
                        none_row += [zero] * size
                    pad = [0] * (width - len(src_row))
                    src_rows.append(src_row + pad)
                    id_rows.append(id_row + pad)
                    none_rows.append(none_row + pad)
        sources.append(src_rows)
        op_ids.append(id_rows)
        nothing = none_rows
    return np.array(sources, np.int32), np.array(op_ids, np.int32), np.array(nothing, np.int32)


def pairs(count, first):
    if first:
        return [(i, i ^ 1) for i in range(count) if (i ^ 1) < count]
    found = []
    for i in range(1, count - 1, 2):
        found += [(i, i + 1), (i + 1, i)]
    return found


def exchange(block, axis, unit, count):
    n = lax.axis_size(axis)
    odd = lax.rem(lax.axis_index(axis), 2)
    got = []
    for first, size in zip((True, False), halo_sizes(count)):
        edge = block
        if size < count:
            low = (1 - odd) if first else odd
            edge = lax.dynamic_slice_in_dim(block, low * ((count - size) * unit), size * unit, 0)
        got.append(lax.ppermute(edge, axis, pairs(n, first)))
    return got


def swap_bits(axis):
    return lax.axis_size(axis).bit_length() - 1


def in_order(block, axis):
    n, bits = lax.axis_size(axis), swap_bits(axis)
    spots = [int(format(s, "0%db" % bits)[::-1], 2) for s in range(n)] if bits else [0]
    at = jnp.asarray(np.array(spots, np.int32))[jnp.arange(n, dtype=jnp.int32) ^ lax.axis_index(axis)]
    block = jnp.take(block, at, axis=0)
    return block.transpose(1, 2, 0, 3).reshape(1, block.shape[1], 2, n * block.shape[3])


def times_i(v, sides):
    sign = jnp.where(lax.broadcasted_iota(jnp.int32, (2 * sides, 1), 0) < sides, -1.0, 1.0)
    return sign.astype(F32) * pltpu.roll(v, sides, 0)


def row_of(ref, lead, part, lane, width, comps):
    return jnp.broadcast_to(ref[(*lead, slice(part, part + 1), pl.ds(lane, width))], (comps, width))


def add_slots(sums, coefs, pieces):
    real, imag = coefs
    for m, piece in enumerate(pieces):
        add = [real * piece, imag * piece]
        sums[m] = add if sums[m] is None else [a + b for a, b in zip(sums[m], add)]


def widen(src, fine, comps):
    count = src.shape[0] // comps
    fine[:count] = src[...].astype(F32).reshape(count, comps, src.shape[1])
    fine[count] = jnp.zeros(fine.shape[1:], F32)


def spread_chunk(src, interp, j, buffer, comps):
    lanes = slice(j * CHUNK, (j + 1) * CHUNK)
    out = jnp.dot(src[...], interp[:, lanes], preferred_element_type=F32)
    buffer[...] = out.reshape(-1, comps, CHUNK)


def shifts(trig, j, comps, width=CHUNK):
    lanes = slice(j * CHUNK, j * CHUNK + width)
    return [jnp.broadcast_to(trig[k : k + 1, lanes], (comps, width)) for k in range(8)]


def aggregate_chunk(buffer, shift, pattern, lanes, width, sides, base=0):
    for q in range(buffer.shape[0] // 4):
        r, c = divmod(q, width)
        total = [None, None]
        for k in range(4):
            piece = buffer[(2 * r + k // 2) * (2 * width) + 2 * c + k % 2]
            for i in range(2):
                add = shift[4 * i + k] * piece
                total[i] = add if k == 0 else total[i] + add
        whole = total[0] + times_i(total[1], sides)
        pattern[base + q, :, lanes] = whole.astype(BF16).astype(F32)


def aggregate(src, interp, trig, buffers, pattern, width, sides, base=0, done=lambda j: None):
    comps = 2 * sides
    steps = interp.shape[1] // CHUNK
    spread_chunk(src, interp, 0, buffers[0], comps)
    for j in range(steps):
        if j + 1 < steps:
            spread_chunk(src, interp, j + 1, buffers[(j + 1) % 2], comps)
        lanes = slice(j * CHUNK, (j + 1) * CHUNK)
        aggregate_chunk(buffers[j % 2], shifts(trig, j, comps), pattern, lanes, width, sides, base)
        done(j)


def zero_box(pattern):
    pattern[pattern.shape[0] - 1] = jnp.zeros(pattern.shape[1:], F32)


def near_sums(table, fops, fine, group, base, op_ids):
    comps, fdirs = fine.shape[1:]
    sums = [None] * len(group)
    for t, op_id in enumerate(op_ids, base):
        coefs = [row_of(fops, (op_id,), i, 0, fdirs, comps) for i in range(2)]
        add_slots(sums, coefs, [fine[table[box, t]] for box in group])
    return [real + times_i(imag, comps // 2) for real, imag in sums]


def near_side(table, ids, fops, fine, rows, cols, base, count, first_col, store):
    for a in range(2):
        for c in range(2):
            group = [(2 * r + a) * (2 * cols) + first_col + c for r in range(rows)]
            op_ids = [ids[group[0], t] for t in range(base, base + count)]
            for r, value in enumerate(near_sums(table, fops, fine, group, base, op_ids)):
                store((2 * r + a) * 2 + c, value)


def block_kernel(rows, cols, sides, table, src, phase, fops, near, trig, fine):
    trig[:4] = jnp.cos(phase[...])
    trig[4:] = jnp.sin(phase[...])
    widen(src, fine, 2 * sides)
    for a in range(2):
        for c in range(2 * cols):
            op_ids = [o for o, _ in fine_slots(a, c, rows, cols, 0, 0)[0]]
            group = [(2 * r + a) * (2 * cols) + c for r in range(rows)]
            for box, value in zip(group, near_sums(table, fops, fine, group, 0, op_ids)):
                near[box] = value


def pack_kernel(rows, cols, sides, own, first, second, after, strip):
    at = 0
    for ref in (own, first, second):
        strip[at : at + ref.shape[0]] = ref[...]
        at += ref.shape[0]


def own_kernel(rows, cols, sides, table, strip, interp, trig, fops, near_block, pattern, near, fine, even, odd):
    base = starts(slot_counts(rows, cols, 2))[1]
    inside = near.shape[0] * 2 * sides
    widen(strip.at[pl.ds(inside, strip.shape[0] - inside)], fine, 2 * sides)
    near[...] = near_block[...]
    aggregate(strip, interp, trig, (even, odd), pattern, cols, sides)
    zero_box(pattern)
    for r in range(2 * rows):
        for c in range(2 * cols):
            op_ids = [o for o, _ in fine_slots(r, c, rows, cols, 0, 0)[1]]
            if op_ids:
                box = r * 2 * cols + c
                near[box] += near_sums(table, fops, fine, [box], base, op_ids)[0]


def side_kernel(rows, cols, sides, table, ids, info, src, interp, trig, fops, pattern, near, fine, even, odd):
    counts = slot_counts(rows, cols, 2)
    widen(src, fine, 2 * sides)

    def store(at, value):
        near[at] = value

    aggregate(src, interp, trig, (even, odd), pattern, halo_sizes(cols)[0], sides)
    zero_box(pattern)
    near_side(
        table, ids, fops, fine, rows, cols, starts(counts)[2], counts[2], info[0, 0] * (2 * cols - 2), store
    )


def parent_groups(rows, cols):
    return [[(r, c) for r in range(start, rows, 2)] for c in range(cols) for start in range(2)]


def parent_sums(rows, cols, sides, table, ids, pops, sources, group, first, width):
    comps = 2 * sides
    rows_at = [4 * rows * cols + r * cols + c for r, c in group]
    sums = [None] * len(group)
    for base, count, ref in sources:
        for t in range(base, base + count):
            op_id = ids[rows_at[0], t]
            coefs = [row_of(pops, (op_id,), i, first, width, comps) for i in range(2)]
            add_slots(sums, coefs, [ref[table[row, t], :, first : first + width] for row in rows_at])
    return sums


def inner_kernel(rows, cols, sides, table, ids, info, pat_own, pat_a, *refs):
    *shards, pops, real, imag = refs
    at = 0
    for ref in shards:
        held = ref.shape[3]
        for k in range(ref.shape[0]):
            lane = pl.multiple_of(info[1, at] * held, held)
            pops[:, :, pl.ds(lane, held)] = ref[k]
            at += 1
    counts = slot_counts(rows, cols, 1)
    at = starts(counts)
    sources = [(at[0], counts[0], pat_own), (at[1], counts[1], pat_a)]
    for first in range(0, real.shape[2], 2 * CHUNK):
        for group in parent_groups(rows, cols):
            sums = parent_sums(
                rows, cols, sides, table, ids, pops, sources, group, first, 2 * CHUNK
            )
            for (r, c), (re, im) in zip(group, sums):
                real[r * cols + c, :, first : first + 2 * CHUNK] = re
                imag[r * cols + c, :, first : first + 2 * CHUNK] = im


def last_kernel(
    rows, cols, sides,
    table, ids, info,
    src, interp, trig, fops, pops, real, imag, near_own, near_a,
    out,
    fine, even, odd, pat_b, child, near_b, acc,
):
    comps, fdirs = fine.shape[1:]
    fcols = 2 * cols
    wide = 2 * CHUNK
    counts = slot_counts(rows, cols, 2)
    par_counts = slot_counts(rows, cols, 1)
    a_right = info[0, 0]
    widen(src, fine, comps)
    zero_box(pat_b)

    def store(at, value):
        near_b[1 - a_right, at] = value

    near_side(
        table, ids, fops, fine, rows, cols, starts(counts)[3], counts[3], (1 - a_right) * (fcols - 2), store
    )
    for at in range(near_a.shape[0]):
        near_b[a_right, at] = near_a[at]

    def far(j):
        if j % 2 == 0:
            return
        first = (j - 1) * CHUNK
        shift = shifts(trig, j - 1, comps, wide)
        sources = [(starts(par_counts)[2], par_counts[2], pat_b)]
        for group in parent_groups(rows, cols):
            sums = parent_sums(rows, cols, sides, table, ids, pops, sources, group, first, wide)
            for (r, c), (re, im) in zip(group, sums):
                box = r * cols + c
                re = re + real[box, :, first : first + wide]
                im = im + imag[box, :, first : first + wide]
                total = (re + times_i(im, sides)).astype(BF16).astype(F32)
                turned = times_i(total, sides)
                for k in range(4):
                    at = (2 * r + k // 2) * fcols + 2 * c + k % 2
                    child[at, :, first : first + wide] = (
                        shift[k] * total - shift[4 + k] * turned
                    ).astype(BF16)
        back = lax.dot_general(
            child[:, :, first : first + wide].reshape(-1, wide), interp[:, first : first + wide],
            (((1,), (1,)), ((), ())), preferred_element_type=F32,
        ).reshape(acc.shape)
        acc[...] = back if j == 1 else acc[...] + back

    aggregate(src, interp, trig, (even, odd), pat_b, halo_sizes(cols)[1], sides, 0, far)

    scale = fdirs / interp.shape[1]
    for r in range(2 * rows):
        for c in range(fcols):
            at = r * fcols + c
            value = near_own[at] + acc[at] * scale
            if c < 2:
                value = value + near_b[0, r * 2 + c]
            if c >= fcols - 2:
                value = value + near_b[1, r * 2 + c - (fcols - 2)]
            out[r, c, 0] = value[:sides]
            out[r, c, 1] = value[sides:]


def per_device(
    fine_out, interp, child_phase, fine_ops, parent_ops, fine_src, fine_op, parent_src, parent_op
):
    frows, fcols, _, sides, fdirs = fine_out.shape
    rows, cols = frows // 2, fcols // 2
    comps = 2 * sides
    pdirs = interp.shape[1]
    assert all(size == cols for size in halo_sizes(cols)) and pdirs % (2 * CHUNK) == 0
    patch_odd = lax.rem(lax.axis_index("patch"), 2)
    dir_at = lax.axis_index("dir")
    dir_odd = lax.rem(dir_at, 2)
    height = rows + sum(halo_sizes(rows))
    boxes = height * cols
    n_dir, bits = lax.axis_size("dir"), swap_bits("dir")

    own = fine_out.reshape(frows * fcols * comps, fdirs)
    shards = [parent_ops[None]]
    for bit in reversed(range(bits)):
        held = jnp.concatenate(shards, axis=0)
        shards.append(lax.ppermute(held, "dir", [(i, i ^ (1 << bit)) for i in range(n_dir)]))
    if parent_ops.shape[2] % 128 == 0:
        places = jnp.arange(n_dir, dtype=jnp.int32)
        spots = dir_at
        for b in range(bits):
            spots = spots ^ (((places >> b) & 1) << (bits - 1 - b))
    else:
        shards = [in_order(jnp.concatenate(shards, axis=0), "dir")]
        spots = jnp.zeros((n_dir,), jnp.int32)
    first_row = lax.broadcasted_iota(jnp.int32, (2, n_dir), 0) == 0
    info = jnp.where(first_row, 1 - dir_odd, spots[None])

    outside = boxes - rows * cols
    sources, op_ids, nothing = build_tables(
        rows, cols, {2: [frows * fcols, 4 * outside, 4 * boxes, 4 * boxes], 1: [boxes] * 3}
    )
    which = patch_odd * 2 + dir_odd
    sources, ids = jnp.asarray(sources)[which], jnp.asarray(op_ids)[which]
    lists = jnp.concatenate([
        lax.dynamic_slice_in_dim(op, dir_at * width, width, 1).reshape(-1, 1, op.shape[2])
        for op, width in ((fine_op, fcols), (parent_op, cols))
    ])
    present = jnp.any(lists == ids[:, :, None], axis=2)
    table = jnp.where(present, sources, jnp.asarray(nothing))

    smem = pl.BlockSpec(memory_space=pltpu.SMEM)
    vmem = pl.BlockSpec(memory_space=pltpu.VMEM)

    def shape(*dims):
        return jax.ShapeDtypeStruct(dims, F32)

    def scratch(*dims, kind=F32):
        return pltpu.VMEM(dims, kind)

    def group_scratch(count):
        return [scratch(count + 1, comps, fdirs)] + [scratch(count, comps, CHUNK)] * 2

    def call(body, name, n_smem, outs, scratches, *args):
        return pl.pallas_call(
            functools.partial(body, rows, cols, sides),
            out_shape=outs,
            in_specs=[smem] * n_smem + [vmem] * (len(args) - n_smem),
            out_specs=[vmem] * len(outs),
            scratch_shapes=scratches,
            compiler_params=pltpu.CompilerParams(vmem_limit_bytes=LIMITS[name] << 20),
            name=name,
        )(*args)

    near = shape(frows * fcols, comps, fdirs)
    pattern = shape(boxes + 1, comps, pdirs)
    patch_halo = exchange(own, "patch", 2 * fcols * comps, rows)
    near_block, trig = call(
        block_kernel, "block", 1, [near, shape(8, pdirs)], [scratch(frows * fcols + 1, comps, fdirs)],
        table, own, child_phase, fine_ops,
    )
    strip = call(
        pack_kernel, "pack", 0,
        [jax.ShapeDtypeStruct((4 * boxes * comps, fdirs), BF16)], [], own, *patch_halo, near_block,
    )[0]
    side_a, side_b = exchange(strip, "dir", 1, cols)
    pat_own, near_own = call(
        own_kernel, "own", 1, [pattern, near],
        [scratch(4 * outside + 1, comps, fdirs)] + [scratch(4 * boxes, comps, CHUNK)] * 2,
        table, strip, interp, trig, fine_ops, near_block,
    )
    pat_a, near_a = call(
        side_kernel, "side", 3, [pattern, shape(frows * 2, comps, fdirs)], group_scratch(4 * boxes),
        table, ids, info, side_a, interp, trig, fine_ops,
    )
    part = shape(rows * cols, comps, pdirs)
    pops, real, imag = call(
        inner_kernel, "inner", 3, [shape(parent_ops.shape[0], 2, pdirs), part, part], [],
        table, ids, info, pat_own, pat_a, *shards,
    )
    return call(
        last_kernel, "last", 3, [jax.ShapeDtypeStruct(fine_out.shape, F32)],
        group_scratch(4 * boxes) + [
            scratch(boxes + 1, comps, pdirs),
            scratch(frows * fcols, comps, pdirs, kind=BF16),
            scratch(2, frows * 2, comps, fdirs),
            scratch(frows * fcols, comps, fdirs),
        ],
        table, ids, info, side_b, interp, trig, fine_ops, pops, real, imag, near_own, near_a,
    )[0]


def solution(mesh):
    in_specs = (
        P("patch", "dir", None, None, None),
        P(),
        P(),
        P(),
        P(None, None, "dir"),
        P("patch", None, None),
        P("patch", None, None),
        P("patch", None, None),
        P("patch", None, None),
    )
    out_specs = P("patch", "dir", None, None, None)
    return jax.shard_map(
        per_device, mesh=mesh, in_specs=in_specs, out_specs=out_specs, check_vma=False
    )
```

```python
import functools

import jax
import jax.numpy as jnp
import numpy as np
from jax import lax
from jax.experimental import pallas as pl
from jax.experimental.pallas import tpu as pltpu
from jax.sharding import PartitionSpec as P

CHUNK = 512
PIECE = 256
LIMITS = {"block": 8, "pack": 4, "edge": 4, "lists": 4, "own": 16, "side": 16, "inner": 12, "last": 24}
F32, BF16 = jnp.float32, jnp.bfloat16


def offset_pairs():
    return [(dr, dc) for dr in range(-3, 4) for dc in range(-3, 4) if max(abs(dr), abs(dc)) > 1]


def class_offsets(row_odd, col_odd):
    return [
        (op_id, dr, dc)
        for op_id, (dr, dc) in enumerate(offset_pairs())
        if -2 <= dr + row_odd <= 3 and -2 <= dc + col_odd <= 3
    ]


def halo_sizes(count):
    return (3, 2) if count % 2 else (2, 2)


def stored_at(rel, count, odd):
    first, second = halo_sizes(count)
    if 0 <= rel < count:
        return rel
    if rel < 0:
        return count + first + rel if odd else count + first + second + rel
    return rel if not odd else rel + first


def place(row, col, rows, cols, row_odd, col_odd, scale):
    at_r = stored_at(row // scale, rows, row_odd) * scale + row % scale
    at_c = stored_at(col // scale, cols, col_odd) * scale + col % scale
    for group, width in enumerate((cols, *halo_sizes(cols))):
        if at_c < width * scale:
            return group, at_r * width * scale + at_c
        at_c -= width * scale


def fine_slots(row, col, rows, cols, row_odd, col_odd):
    inside, found = 4 * rows * cols, ([], [], [], [])
    for op_id, dr, dc in class_offsets(row % 2, col % 2):
        group, index = place(row + dr, col + dc, rows, cols, row_odd, col_odd, 2)
        if group:
            found[group + 1].append((op_id, index))
        elif index >= inside:
            found[0].append((op_id, None))
            found[1].append((op_id, index - inside))
        else:
            found[0].append((op_id, index))
    return found


def parent_slots(row, col, rows, cols, row_odd, col_odd):
    found = ([], [], [])
    for op_id, dr, dc in class_offsets((row + row_odd * rows) % 2, (col + col_odd * cols) % 2):
        group, index = place(row + dr, col + dc, rows, cols, row_odd, col_odd, 1)
        found[group].append((op_id, index))
    return found


PARITIES = [(a, b) for a in range(2) for b in range(2)]


def slot_counts(rows, cols, scale):
    slots = fine_slots if scale == 2 else parent_slots
    lists = [
        [len(found) for found in slots(r, c, rows, cols, *odd)]
        for odd in PARITIES for r in range(rows * scale) for c in range(cols * scale)
    ]
    most = [max(column) for column in zip(*lists)]
    return most[:-2] + [max(most[-2:])] * 2


def starts(counts):
    return [sum(counts[:i]) for i in range(len(counts))]


def build_tables(rows, cols, zeros):
    counts = {scale: slot_counts(rows, cols, scale) for scale in (2, 1)}
    width = max(sum(c) for c in counts.values())
    sources, op_ids, nothing = [], [], []
    for odd in PARITIES:
        src_rows, id_rows, none_rows = [], [], []
        for scale, slots in ((2, fine_slots), (1, parent_slots)):
            for r in range(rows * scale):
                for c in range(cols * scale):
                    src_row, id_row, none_row = [], [], []
                    for size, found, zero in zip(counts[scale], slots(r, c, rows, cols, *odd), zeros[scale]):
                        found = found + [(0, None)] * (size - len(found))
                        src_row += [zero if at is None else at for _, at in found]
                        id_row += [o for o, _ in found]
                        none_row += [zero] * size
                    pad = [0] * (width - len(src_row))
                    src_rows.append(src_row + pad)
                    id_rows.append(id_row + pad)
                    none_rows.append(none_row + pad)
        sources.append(src_rows)
        op_ids.append(id_rows)
        nothing = none_rows
    return np.array(sources, np.int32), np.array(op_ids, np.int32), np.array(nothing, np.int32)


def shared_ids(op_ids, rows, cols):
    fine, par = slot_counts(rows, cols, 2), slot_counts(rows, cols, 1)
    width = max(2 * fine[2], sum(par))
    found = []
    for which, (_, dir_odd) in enumerate(PARITIES):
        entries = []
        for a in range(2):
            for c in range(2):
                entry = []
                for group, right in ((2, 1 - dir_odd), (3, dir_odd)):
                    box = a * 2 * cols + right * (2 * cols - 2) + c
                    at = starts(fine)[group]
                    entry += list(op_ids[which, box, at : at + fine[group]])
                entries.append(entry)
        for c in range(cols):
            for start in range(2):
                entries.append(list(op_ids[which, 4 * rows * cols + start * cols + c, : sum(par)]))
        found.append([entry + [0] * (width - len(entry)) for entry in entries])
    return np.array(found, np.int32)


def parity(axis):
    return lax.rem(lax.axis_index(axis), 2)


def parities():
    return parity("patch") * 2 + parity("dir")


def pairs(count, first):
    if first:
        return [(i, i ^ 1) for i in range(count) if (i ^ 1) < count]
    found = []
    for i in range(1, count - 1, 2):
        found += [(i, i + 1), (i + 1, i)]
    return found


def exchange(blocks, axis):
    n = lax.axis_size(axis)
    return [lax.ppermute(block, axis, pairs(n, first)) for block, first in zip(blocks, (True, False))]


def swap_bits(axis):
    return lax.axis_size(axis).bit_length() - 1


def shard_order(axis):
    bits = swap_bits(axis)
    return [int(format(e, "0%db" % bits)[::-1], 2) if bits else 0 for e in range(lax.axis_size(axis))]


def in_order(block, axis):
    n = lax.axis_size(axis)
    at = jnp.asarray(np.array(shard_order(axis), np.int32))[jnp.arange(n, dtype=jnp.int32) ^ lax.axis_index(axis)]
    block = jnp.take(block, at, axis=0)
    return block.transpose(1, 2, 0, 3).reshape(1, block.shape[1], 2, n * block.shape[3])


def times_i(v, sides):
    sign = jnp.where(lax.broadcasted_iota(jnp.int32, (2 * sides, 1), 0) < sides, -1.0, 1.0)
    return sign.astype(F32) * pltpu.roll(v, sides, 0)


def row_of(ref, lead, part, lane, width, comps):
    return jnp.broadcast_to(ref[(*lead, slice(part, part + 1), pl.ds(lane, width))], (comps, width))


def add_slots(sums, coefs, pieces):
    real, imag = coefs
    for m, piece in enumerate(pieces):
        add = [real * piece, imag * piece]
        sums[m] = add if sums[m] is None else [a + b for a, b in zip(sums[m], add)]


def widen(src, fine, comps):
    count = src.shape[0] // comps
    fine[:count] = src[...].astype(F32).reshape(count, comps, src.shape[1])
    fine[count] = jnp.zeros(fine.shape[1:], F32)


def spread_chunk(src, interp, j, buffer, comps):
    lanes = slice(j * CHUNK, (j + 1) * CHUNK)
    out = jnp.dot(src[...], interp[:, lanes], preferred_element_type=F32)
    buffer[...] = out.reshape(-1, comps, CHUNK)


def shifts(trig, j, comps):
    lanes = slice(j * CHUNK, (j + 1) * CHUNK)
    return [jnp.broadcast_to(trig[k : k + 1, lanes], (comps, CHUNK)) for k in range(8)]


def aggregate_chunk(buffer, trig, j, pattern, width, sides):
    comps = 2 * sides
    for at in range(0, CHUNK, PIECE):
        lanes = slice(j * CHUNK + at, j * CHUNK + at + PIECE)
        shift = [jnp.broadcast_to(trig[k : k + 1, lanes], (comps, PIECE)) for k in range(8)]
        for q in range(buffer.shape[0] // 4):
            r, c = divmod(q, width)
            total = [None, None]
            for k in range(4):
                piece = buffer[(2 * r + k // 2) * (2 * width) + 2 * c + k % 2, :, at : at + PIECE]
                for i in range(2):
                    add = shift[4 * i + k] * piece
                    total[i] = add if k == 0 else total[i] + add
            whole = total[0] + times_i(total[1], sides)
            pattern[q, :, lanes] = whole.astype(BF16).astype(F32)


def aggregate(src, interp, trig, buffers, pattern, width, sides, beside=lambda j: None, done=lambda j: None):
    comps = 2 * sides
    steps = interp.shape[1] // CHUNK
    spread_chunk(src, interp, 0, buffers[0], comps)
    for j in range(steps):
        if j + 1 < steps:
            spread_chunk(src, interp, j + 1, buffers[(j + 1) % 2], comps)
        beside(j)
        aggregate_chunk(buffers[j % 2], trig, j, pattern, width, sides)
        done(j)


def dealt(items, j, steps):
    return items[len(items) * j // steps : len(items) * (j + 1) // steps]


def zero_box(pattern):
    pattern[pattern.shape[0] - 1] = jnp.zeros(pattern.shape[1:], F32)


def near_sums(table, fops, fine, group, base, op_ids):
    comps, fdirs = fine.shape[1:]
    sums = [None] * len(group)
    for t, op_id in enumerate(op_ids, base):
        coefs = [row_of(fops, (op_id,), i, 0, fdirs, comps) for i in range(2)]
        add_slots(sums, coefs, [fine[table[box, t]] for box in group])
    return [real + times_i(imag, comps // 2) for real, imag in sums]


def near_side(table, ids, fops, fine, rows, cols, group, right, store, classes):
    counts = slot_counts(rows, cols, 2)
    base, count, which = starts(counts)[group], counts[group], parities()
    first_col = right * (2 * cols - 2)
    for a, c in classes:
        boxes = [(2 * r + a) * (2 * cols) + first_col + c for r in range(rows)]
        op_ids = [ids[which, 2 * a + c, (group - 2) * count + t] for t in range(count)]
        for r, value in enumerate(near_sums(table, fops, fine, boxes, base, op_ids)):
            store((2 * r + a) * 2 + c, value)


def block_kernel(rows, cols, sides, table, src, phase, fops, near, trig, fine):
    half = phase.shape[1] // 2
    both = jnp.concatenate([phase[:, :half], phase[:, half:]], axis=0)
    for first, wave in ((0, jnp.cos(both)), (4, jnp.sin(both))):
        trig[first : first + 4, :half] = wave[:4]
        trig[first : first + 4, half:] = wave[4:]
    widen(src, fine, 2 * sides)
    for a in range(2):
        for c in range(2 * cols):
            op_ids = [o for o, _ in fine_slots(a, c, rows, cols, 0, 0)[0]]
            group = [(2 * r + a) * (2 * cols) + c for r in range(rows)]
            for box, value in zip(group, near_sums(table, fops, fine, group, 0, op_ids)):
                near[box] = value


def lists_kernel(rows, cols, sides, fine_op, par_op, lists, table):
    which = parities()
    at, boxes = 0, table.shape[0]
    for op, scale, none in ((fine_op, 2, 2 * boxes), (par_op, 1, 2 * boxes + 1)):
        across = cols * scale
        first = pl.multiple_of(lax.axis_index("dir") * across, across)
        for r in range(rows * scale):
            mine = op[r, pl.ds(first, across), :]
            wanted = lists[which, boxes + at : boxes + at + across]
            found = mine[:, 0:1] == wanted
            for slot in range(1, op.shape[2]):
                found = found | (mine[:, slot : slot + 1] == wanted)
            zero = jnp.broadcast_to(lists[which, none : none + 1], wanted.shape)
            table[at : at + across] = jnp.where(found, lists[which, at : at + across], zero)
            at += across


def edge_kernel(rows, cols, sides, own, edge):
    size = halo_sizes(rows)[1]
    unit = own.shape[0] // rows
    at = pl.multiple_of(parity("patch") * ((rows - size) * unit), unit)
    edge[...] = own[pl.ds(at, size * unit)]


def pack_kernel(rows, cols, sides, own, first, second, after, strip):
    at = 0
    for ref in (own, first, second):
        strip[at : at + ref.shape[0]] = ref[...]
        at += ref.shape[0]


def own_kernel(rows, cols, sides, table, strip, interp, trig, fops, near_block, pattern, near, fine, even, odd):
    base = starts(slot_counts(rows, cols, 2))[1]
    inside = near.shape[0] * 2 * sides
    widen(strip.at[pl.ds(inside, strip.shape[0] - inside)], fine, 2 * sides)
    steps = interp.shape[1] // CHUNK

    def beside(j):
        for box in dealt(range(near.shape[0]), j, min(steps, 2)) if j < 2 else ():
            op_ids = [o for o, _ in fine_slots(*divmod(box, 2 * cols), rows, cols, 0, 0)[1]]
            more = near_sums(table, fops, fine, [box], base, op_ids)[0] if op_ids else 0.0
            near[box] = near_block[box] + more

    aggregate(strip, interp, trig, (even, odd), pattern, cols, sides, beside)
    zero_box(pattern)


def side_kernel(rows, cols, sides, table, ids, src, interp, trig, fops, pattern, near, fine, even, odd):
    widen(src, fine, 2 * sides)

    def store(at, value):
        near[at] = value

    steps = interp.shape[1] // CHUNK

    def beside(j):
        near_side(table, ids, fops, fine, rows, cols, 2, 1 - parity("dir"), store, dealt(PARITIES, j, steps))

    aggregate(src, interp, trig, (even, odd), pattern, halo_sizes(cols)[0], sides, beside)
    zero_box(pattern)


def parent_groups(rows, cols):
    return [[(r, c) for r in range(start, rows, 2)] for c in range(cols) for start in range(2)]


def parent_sums(rows, cols, sides, table, ids, pops, sources, index, group, first, width):
    comps, which = 2 * sides, parities()
    rows_at = [4 * rows * cols + r * cols + c for r, c in group]
    sums = [None] * len(group)
    for base, count, ref in sources:
        for t in range(base, base + count):
            op_id = ids[which, 4 + index, t]
            coefs = [row_of(pops, (op_id,), i, first, width, comps) for i in range(2)]
            add_slots(sums, coefs, [ref[table[row, t], :, first : first + width] for row in rows_at])
    return sums


def inner_kernel(rows, cols, sides, table, ids, pat_own, pat_a, *refs):
    *shards, pops, real, imag = refs
    at = 0
    for ref in shards:
        held = ref.shape[3]
        for k in range(ref.shape[0]):
            lane = pl.multiple_of((shard_order("dir")[at] ^ lax.axis_index("dir")) * held, held) if held < pops.shape[2] else 0
            pops[:, :, pl.ds(lane, held)] = ref[k]
            at += 1
    counts = slot_counts(rows, cols, 1)
    at = starts(counts)
    sources = [(at[0], counts[0], pat_own), (at[1], counts[1], pat_a)]
    for first in range(0, real.shape[2], 2 * CHUNK):
        for index, group in enumerate(parent_groups(rows, cols)):
            sums = parent_sums(
                rows, cols, sides, table, ids, pops, sources, index, group, first, 2 * CHUNK
            )
            for (r, c), (re, im) in zip(group, sums):
                real[r * cols + c, :, first : first + 2 * CHUNK] = re
                imag[r * cols + c, :, first : first + 2 * CHUNK] = im


def last_kernel(
    rows, cols, sides,
    table, ids,
    src, interp, trig, fops, pops, real, imag, near_own, near_a,
    out,
    fine, even, odd, pat_b, child, near_b, acc,
):
    comps, fdirs = fine.shape[1:]
    fcols = 2 * cols
    par_counts = slot_counts(rows, cols, 1)
    a_right = 1 - parity("dir")
    widen(src, fine, comps)
    zero_box(pat_b)

    def store(at, value):
        near_b[1 - a_right, at] = value

    for at in range(near_a.shape[0]):
        near_b[a_right, at] = near_a[at]
    steps = interp.shape[1] // CHUNK

    def beside(j):
        near_side(table, ids, fops, fine, rows, cols, 3, 1 - a_right, store, dealt(PARITIES, j, steps))

    def back(j):
        lanes = slice(j * CHUNK, (j + 1) * CHUNK)
        more = lax.dot_general(
            child[:, :, lanes].reshape(-1, CHUNK), interp[:, lanes],
            (((1,), (1,)), ((), ())), preferred_element_type=F32,
        ).reshape(acc.shape)
        acc[...] = more if j == 0 else acc[...] + more

    def far(j):
        if j:
            back(j - 1)
        lanes = slice(j * CHUNK, (j + 1) * CHUNK)
        shift = shifts(trig, j, comps)
        sources = [(starts(par_counts)[2], par_counts[2], pat_b)]
        for index, group in enumerate(parent_groups(rows, cols)):
            sums = parent_sums(rows, cols, sides, table, ids, pops, sources, index, group, j * CHUNK, CHUNK)
            for (r, c), (re, im) in zip(group, sums):
                box = r * cols + c
                total = re + real[box, :, lanes] + times_i(im + imag[box, :, lanes], sides)
                total = total.astype(BF16).astype(F32)
                turned = times_i(total, sides)
                for k in range(4):
                    at = (2 * r + k // 2) * fcols + 2 * c + k % 2
                    child[at, :, lanes] = (shift[k] * total - shift[4 + k] * turned).astype(BF16)

    aggregate(src, interp, trig, (even, odd), pat_b, halo_sizes(cols)[1], sides, beside, far)
    back(steps - 1)

    scale = fdirs / interp.shape[1]
    for r in range(2 * rows):
        for c in range(fcols):
            at = r * fcols + c
            value = near_own[at] + acc[at] * scale
            if c < 2:
                value = value + near_b[0, r * 2 + c]
            if c >= fcols - 2:
                value = value + near_b[1, r * 2 + c - (fcols - 2)]
            out[r, c, 0] = value[:sides]
            out[r, c, 1] = value[sides:]


def per_device(
    fine_out, interp, child_phase, fine_ops, parent_ops, fine_src, fine_op, parent_src, parent_op
):
    frows, fcols, _, sides, fdirs = fine_out.shape
    rows, cols = frows // 2, fcols // 2
    comps = 2 * sides
    pdirs = interp.shape[1]
    assert all(size == cols for size in halo_sizes(cols)) and pdirs % (2 * CHUNK) == 0
    height = rows + sum(halo_sizes(rows))
    boxes = height * cols
    n_dir, bits = lax.axis_size("dir"), swap_bits("dir")

    own = fine_out.reshape(frows * fcols * comps, fdirs)
    outside = boxes - rows * cols
    sources, op_ids, nothing = build_tables(
        rows, cols, {2: [frows * fcols, 4 * outside, 4 * boxes, 4 * boxes], 1: [boxes] * 3}
    )
    ids = jnp.asarray(shared_ids(op_ids, rows, cols))
    nothing = np.broadcast_to(nothing[[0, -1]], (len(PARITIES), 2, nothing.shape[1]))
    lists = jnp.asarray(np.concatenate([sources, op_ids, nothing], axis=1))

    smem = pl.BlockSpec(memory_space=pltpu.SMEM)
    vmem = pl.BlockSpec(memory_space=pltpu.VMEM)

    def shape(*dims):
        return jax.ShapeDtypeStruct(dims, F32)

    def scratch(*dims, kind=F32):
        return pltpu.VMEM(dims, kind)

    def group_scratch(count):
        return [scratch(count + 1, comps, fdirs)] + [scratch(count, comps, CHUNK)] * 2

    def call(body, name, n_smem, outs, scratches, *args):
        return pl.pallas_call(
            functools.partial(body, rows, cols, sides),
            out_shape=outs,
            in_specs=[smem] * n_smem + [vmem] * (len(args) - n_smem),
            out_specs=[vmem] * len(outs),
            scratch_shapes=scratches,
            compiler_params=pltpu.CompilerParams(vmem_limit_bytes=LIMITS[name] << 20),
            name=name,
        )(*args)

    near = shape(frows * fcols, comps, fdirs)
    pattern = shape(boxes + 1, comps, pdirs)
    table = call(
        lists_kernel, "lists", 0, [jax.ShapeDtypeStruct(sources.shape[1:], jnp.int32)], [],
        fine_op, parent_op, lists,
    )[0]
    first, second = halo_sizes(rows)
    assert first == rows
    edge = call(
        edge_kernel, "edge", 0,
        [jax.ShapeDtypeStruct((own.shape[0] // rows * second, fdirs), BF16)], [], own,
    )[0]
    patch_halo = exchange([own, edge], "patch")
    shards = [parent_ops[None]]
    for bit in reversed(range(bits)):
        held = jnp.concatenate(shards, axis=0)
        shards.append(lax.ppermute(held, "dir", [(i, i ^ (1 << bit)) for i in range(n_dir)]))
    near_block, trig = call(
        block_kernel, "block", 1, [near, shape(8, pdirs)], [scratch(frows * fcols + 1, comps, fdirs)],
        table, own, child_phase, fine_ops,
    )
    strip = call(
        pack_kernel, "pack", 0,
        [jax.ShapeDtypeStruct((4 * boxes * comps, fdirs), BF16)], [], own, *patch_halo, near_block,
    )[0]
    side_a, side_b = exchange([strip, strip], "dir")
    if parent_ops.shape[2] % 128:
        shards = [in_order(jnp.concatenate(shards, axis=0), "dir")]
    pat_own, near_own = call(
        own_kernel, "own", 1, [pattern, near],
        [scratch(4 * outside + 1, comps, fdirs)] + [scratch(4 * boxes, comps, CHUNK)] * 2,
        table, strip, interp, trig, fine_ops, near_block,
    )
    pat_a, near_a = call(
        side_kernel, "side", 2, [pattern, shape(frows * 2, comps, fdirs)], group_scratch(4 * boxes),
        table, ids, side_a, interp, trig, fine_ops,
    )
    part = shape(rows * cols, comps, pdirs)
    pops, real, imag = call(
        inner_kernel, "inner", 2, [shape(parent_ops.shape[0], 2, pdirs), part, part], [],
        table, ids, pat_own, pat_a, *shards,
    )
    return call(
        last_kernel, "last", 2, [jax.ShapeDtypeStruct(fine_out.shape, F32)],
        group_scratch(4 * boxes) + [
            scratch(boxes + 1, comps, pdirs),
            scratch(frows * fcols, comps, pdirs, kind=BF16),
            scratch(2, frows * 2, comps, fdirs),
            scratch(frows * fcols, comps, fdirs),
        ],
        table, ids, side_b, interp, trig, fine_ops, pops, real, imag, near_own, near_a,
    )[0]


def solution(mesh):
    in_specs = (
        P("patch", "dir", None, None, None),
        P(),
        P(),
        P(),
        P(None, None, "dir"),
        P("patch", None, None),
        P("patch", None, None),
        P("patch", None, None),
        P("patch", None, None),
    )
    out_specs = P("patch", "dir", None, None, None)
    return jax.shard_map(
        per_device, mesh=mesh, in_specs=in_specs, out_specs=out_specs, check_vma=False
    )
```

```python
import functools

import jax
import jax.numpy as jnp
import numpy as np
from jax import lax
from jax.experimental import pallas as pl
from jax.experimental.pallas import tpu as pltpu
from jax.sharding import PartitionSpec as P

CHUNK = 512
PIECE = 256
LIMITS = {"block": 8, "pack": 4, "edge": 4, "lists": 4, "both": 20, "inner": 12, "last": 24}
F32, BF16 = jnp.float32, jnp.bfloat16


def offset_pairs():
    return [(dr, dc) for dr in range(-3, 4) for dc in range(-3, 4) if max(abs(dr), abs(dc)) > 1]


def class_offsets(row_odd, col_odd):
    return [
        (op_id, dr, dc)
        for op_id, (dr, dc) in enumerate(offset_pairs())
        if -2 <= dr + row_odd <= 3 and -2 <= dc + col_odd <= 3
    ]


def halo_sizes(count):
    return (3, 2) if count % 2 else (2, 2)


def stored_at(rel, count, odd):
    first, second = halo_sizes(count)
    if 0 <= rel < count:
        return rel
    if rel < 0:
        return count + first + rel if odd else count + first + second + rel
    return rel if not odd else rel + first


def place(row, col, rows, cols, row_odd, col_odd, scale):
    at_r = stored_at(row // scale, rows, row_odd) * scale + row % scale
    at_c = stored_at(col // scale, cols, col_odd) * scale + col % scale
    for group, width in enumerate((cols, *halo_sizes(cols))):
        if at_c < width * scale:
            return group, at_r * width * scale + at_c
        at_c -= width * scale


def fine_slots(row, col, rows, cols, row_odd, col_odd):
    inside, found = 4 * rows * cols, ([], [], [], [])
    for op_id, dr, dc in class_offsets(row % 2, col % 2):
        group, index = place(row + dr, col + dc, rows, cols, row_odd, col_odd, 2)
        if group:
            found[group + 1].append((op_id, index))
        elif index >= inside:
            found[0].append((op_id, None))
            found[1].append((op_id, index - inside))
        else:
            found[0].append((op_id, index))
    return found


def parent_slots(row, col, rows, cols, row_odd, col_odd):
    found = ([], [], [])
    for op_id, dr, dc in class_offsets((row + row_odd * rows) % 2, (col + col_odd * cols) % 2):
        group, index = place(row + dr, col + dc, rows, cols, row_odd, col_odd, 1)
        found[group].append((op_id, index))
    return found


PARITIES = [(a, b) for a in range(2) for b in range(2)]


def slot_counts(rows, cols, scale):
    slots = fine_slots if scale == 2 else parent_slots
    lists = [
        [len(found) for found in slots(r, c, rows, cols, *odd)]
        for odd in PARITIES for r in range(rows * scale) for c in range(cols * scale)
    ]
    most = [max(column) for column in zip(*lists)]
    return most[:-2] + [max(most[-2:])] * 2


def starts(counts):
    return [sum(counts[:i]) for i in range(len(counts))]


def build_tables(rows, cols, zeros):
    counts = {scale: slot_counts(rows, cols, scale) for scale in (2, 1)}
    width = max(sum(c) for c in counts.values())
    sources, op_ids, nothing = [], [], []
    for odd in PARITIES:
        src_rows, id_rows, none_rows = [], [], []
        for scale, slots in ((2, fine_slots), (1, parent_slots)):
            for r in range(rows * scale):
                for c in range(cols * scale):
                    src_row, id_row, none_row = [], [], []
                    for size, found, zero in zip(counts[scale], slots(r, c, rows, cols, *odd), zeros[scale]):
                        found = found + [(0, None)] * (size - len(found))
                        src_row += [zero if at is None else at for _, at in found]
                        id_row += [o for o, _ in found]
                        none_row += [zero] * size
                    pad = [0] * (width - len(src_row))
                    src_rows.append(src_row + pad)
                    id_rows.append(id_row + pad)
                    none_rows.append(none_row + pad)
        sources.append(src_rows)
        op_ids.append(id_rows)
        nothing = none_rows
    return np.array(sources, np.int32), np.array(op_ids, np.int32), np.array(nothing, np.int32)


def shared_ids(op_ids, rows, cols):
    fine, par = slot_counts(rows, cols, 2), slot_counts(rows, cols, 1)
    width = max(2 * fine[2], sum(par))
    found = []
    for which, (_, dir_odd) in enumerate(PARITIES):
        entries = []
        for a in range(2):
            for c in range(2):
                entry = []
                for group, right in ((2, 1 - dir_odd), (3, dir_odd)):
                    box = a * 2 * cols + right * (2 * cols - 2) + c
                    at = starts(fine)[group]
                    entry += list(op_ids[which, box, at : at + fine[group]])
                entries.append(entry)
        for c in range(cols):
            for start in range(2):
                entries.append(list(op_ids[which, 4 * rows * cols + start * cols + c, : sum(par)]))
        found.append([entry + [0] * (width - len(entry)) for entry in entries])
    return np.array(found, np.int32)


def parity(axis):
    return lax.rem(lax.axis_index(axis), 2)


def parities():
    return parity("patch") * 2 + parity("dir")


def pairs(count, first):
    if first:
        return [(i, i ^ 1) for i in range(count) if (i ^ 1) < count]
    found = []
    for i in range(1, count - 1, 2):
        found += [(i, i + 1), (i + 1, i)]
    return found


def exchange(blocks, axis):
    n = lax.axis_size(axis)
    return [lax.ppermute(block, axis, pairs(n, first)) for block, first in zip(blocks, (True, False))]


def swap_bits(axis):
    return lax.axis_size(axis).bit_length() - 1


def shard_order(axis):
    bits = swap_bits(axis)
    return [int(format(e, "0%db" % bits)[::-1], 2) if bits else 0 for e in range(lax.axis_size(axis))]


def in_order(block, axis):
    n = lax.axis_size(axis)
    at = jnp.asarray(np.array(shard_order(axis), np.int32))[jnp.arange(n, dtype=jnp.int32) ^ lax.axis_index(axis)]
    block = jnp.take(block, at, axis=0)
    return block.transpose(1, 2, 0, 3).reshape(1, block.shape[1], 2, n * block.shape[3])


def times_i(v, sides):
    sign = jnp.where(lax.broadcasted_iota(jnp.int32, (2 * sides, 1), 0) < sides, -1.0, 1.0)
    return sign.astype(F32) * pltpu.roll(v, sides, 0)


def row_of(ref, lead, part, lane, width, comps):
    return jnp.broadcast_to(ref[(*lead, slice(part, part + 1), pl.ds(lane, width))], (comps, width))


def add_slots(sums, coefs, pieces):
    real, imag = coefs
    for m, piece in enumerate(pieces):
        add = [real * piece, imag * piece]
        sums[m] = add if sums[m] is None else [a + b for a, b in zip(sums[m], add)]


def widen(src, fine, comps):
    count = src.shape[0] // comps
    fine[:count] = src[...].astype(F32).reshape(count, comps, src.shape[1])
    fine[count] = jnp.zeros(fine.shape[1:], F32)


def spread_chunk(src, interp, j, buffer, comps):
    lanes = slice(j * CHUNK, (j + 1) * CHUNK)
    out = jnp.dot(src[...], interp[:, lanes], preferred_element_type=F32)
    buffer[...] = out.reshape(-1, comps, CHUNK)


def in_steps(steps):
    for tasks in steps:
        for task in tasks:
            task()


def shift_rows(trig, lanes, comps):
    width = lanes.stop - lanes.start
    sign = jnp.where(lax.broadcasted_iota(jnp.int32, (comps, 1), 0) < comps // 2, 1.0, -1.0).astype(F32)
    rows = [jnp.broadcast_to(trig[k : k + 1, lanes], (comps, width)) for k in range(8)]
    return rows[:4], [sign * row for row in rows[4:]]


def aggregate_chunk(buffer, trig, j, pattern, width, sides):
    comps = 2 * sides
    for at in range(0, CHUNK, PIECE):
        lanes = slice(j * CHUNK + at, j * CHUNK + at + PIECE)
        shift = shift_rows(trig, lanes, comps)
        for q in range(buffer.shape[0] // 4):
            r, c = divmod(q, width)
            total = [None, None]
            for k in range(4):
                piece = buffer[(2 * r + k // 2) * (2 * width) + 2 * c + k % 2, :, at : at + PIECE]
                for i in range(2):
                    add = shift[i][k] * piece
                    total[i] = add if k == 0 else total[i] + add
            whole = total[0] + pltpu.roll(total[1], sides, 0)
            pattern[q, :, lanes] = whole.astype(BF16).astype(F32)


def aggregate_tasks(src, interp, trig, buffers, pattern, width, sides):
    steps = range(interp.shape[1] // CHUNK)
    spread = [
        functools.partial(spread_chunk, src, interp, j, buffers[j % 2], 2 * sides) for j in steps
    ]
    sums = [
        functools.partial(aggregate_chunk, buffers[j % 2], trig, j, pattern, width, sides) for j in steps
    ]
    return spread, sums


def dealt(items, j, steps):
    return items[len(items) * j // steps : len(items) * (j + 1) // steps]


def zero_box(pattern):
    pattern[pattern.shape[0] - 1] = jnp.zeros(pattern.shape[1:], F32)


def near_sums(table, fops, fine, group, base, op_ids):
    comps, fdirs = fine.shape[1:]
    sums = [None] * len(group)
    for t, op_id in enumerate(op_ids, base):
        coefs = [row_of(fops, (op_id,), i, 0, fdirs, comps) for i in range(2)]
        add_slots(sums, coefs, [fine[table[box, t]] for box in group])
    return [real + times_i(imag, comps // 2) for real, imag in sums]


def near_side(table, fops, fine, rows, cols, group, right, store, classes):
    counts = slot_counts(rows, cols, 2)
    base, count = starts(counts)[group], counts[group]
    first_col = right * (2 * cols - 2)
    for a, c in classes:
        boxes = [(2 * r + a) * (2 * cols) + first_col + c for r in range(rows)]
        op_ids = [table[5 * rows * cols + 2 * a + c, (group - 2) * count + t] for t in range(count)]
        for r, value in enumerate(near_sums(table, fops, fine, boxes, base, op_ids)):
            store((2 * r + a) * 2 + c, value)


def block_kernel(rows, cols, sides, table, src, phase, fops, near, trig, fine):
    half = phase.shape[1] // 2
    both = jnp.concatenate([phase[:, :half], phase[:, half:]], axis=0)
    for first, wave in ((0, jnp.cos(both)), (4, jnp.sin(both))):
        trig[first : first + 4, :half] = wave[:4]
        trig[first : first + 4, half:] = wave[4:]
    widen(src, fine, 2 * sides)
    for a in range(2):
        for c in range(2 * cols):
            op_ids = [o for o, _ in fine_slots(a, c, rows, cols, 0, 0)[0]]
            group = [(2 * r + a) * (2 * cols) + c for r in range(rows)]
            for box, value in zip(group, near_sums(table, fops, fine, group, 0, op_ids)):
                near[box] = value


def lists_kernel(rows, cols, sides, fine_op, par_op, lists, table):
    which = parities()
    at, boxes = 0, 5 * rows * cols
    table[boxes:] = lists[which, 2 * boxes + 2 :]
    for op, scale, none in ((fine_op, 2, 2 * boxes), (par_op, 1, 2 * boxes + 1)):
        across = cols * scale
        first = pl.multiple_of(lax.axis_index("dir") * across, across)
        for r in range(rows * scale):
            mine = op[r, pl.ds(first, across), :]
            wanted = lists[which, boxes + at : boxes + at + across]
            found = mine[:, 0:1] == wanted
            for slot in range(1, op.shape[2]):
                found = found | (mine[:, slot : slot + 1] == wanted)
            zero = jnp.broadcast_to(lists[which, none : none + 1], wanted.shape)
            table[at : at + across] = jnp.where(found, lists[which, at : at + across], zero)
            at += across


def edge_kernel(rows, cols, sides, own, edge):
    size = halo_sizes(rows)[1]
    unit = own.shape[0] // rows
    at = pl.multiple_of(parity("patch") * ((rows - size) * unit), unit)
    edge[...] = own[pl.ds(at, size * unit)]


def pack_kernel(rows, cols, sides, own, first, second, after, strip):
    at = 0
    for ref in (own, first, second):
        strip[at : at + ref.shape[0]] = ref[...]
        at += ref.shape[0]


def both_kernel(
    rows, cols, sides, table, strip, side_a, interp, trig, fops, near_block,
    pat_own, near, pat_a, near_a, fine, fine_a, even, odd,
):
    base = starts(slot_counts(rows, cols, 2))[1]
    inside = near.shape[0] * 2 * sides
    buffers = (even, odd)
    steps = interp.shape[1] // CHUNK

    def halo(boxes):
        for box in boxes:
            op_ids = [o for o, _ in fine_slots(*divmod(box, 2 * cols), rows, cols, 0, 0)[1]]
            more = near_sums(table, fops, fine, [box], base, op_ids)[0] if op_ids else 0.0
            near[box] = near_block[box] + more

    def store(at, value):
        near_a[at] = value

    def beside(classes):
        near_side(table, fops, fine_a, rows, cols, 2, 1 - parity("dir"), store, classes)

    widen(strip.at[pl.ds(inside, strip.shape[0] - inside)], fine, 2 * sides)
    widen(side_a, fine_a, 2 * sides)
    zero_box(pat_own)
    zero_box(pat_a)
    boxes = strip.shape[0] // (2 * sides)
    whole = jnp.concatenate([strip[...], side_a[...]], axis=0)
    for j in range(steps + 1):
        if j < steps:
            spread_chunk(whole, interp, j, buffers[j % 2], 2 * sides)
        if j < 2:
            beside(PARITIES[2 * j : 2 * j + 2])
        if j in (2, 3):
            halo(dealt(range(near.shape[0]), j - 2, 2))
        if j:
            buffer = buffers[(j - 1) % 2]
            aggregate_chunk(buffer.at[pl.ds(0, boxes)], trig, j - 1, pat_own, cols, sides)
            aggregate_chunk(buffer.at[pl.ds(boxes, boxes)], trig, j - 1, pat_a, halo_sizes(cols)[0], sides)


def parent_groups(rows, cols):
    return [[(r, c) for r in range(start, rows, 2)] for c in range(cols) for start in range(2)]


def parent_sums(rows, cols, sides, table, pops, sources, index, group, first, width):
    comps = 2 * sides
    rows_at = [4 * rows * cols + r * cols + c for r, c in group]
    sums = [None] * len(group)
    for base, count, ref in sources:
        for t in range(base, base + count):
            op_id = table[5 * rows * cols + 4 + index, t]
            coefs = [row_of(pops, (op_id,), i, first, width, comps) for i in range(2)]
            add_slots(sums, coefs, [ref[table[row, t], :, first : first + width] for row in rows_at])
    return sums


def inner_kernel(rows, cols, sides, table, pat_own, pat_a, *refs):
    *shards, pops, real, imag = refs
    at = 0
    for ref in shards:
        held = ref.shape[3]
        for k in range(ref.shape[0]):
            lane = pl.multiple_of((shard_order("dir")[at] ^ lax.axis_index("dir")) * held, held) if held < pops.shape[2] else 0
            pops[:, :, pl.ds(lane, held)] = ref[k]
            at += 1
    counts = slot_counts(rows, cols, 1)
    at = starts(counts)
    sources = [(at[0], counts[0], pat_own), (at[1], counts[1], pat_a)]
    for first in range(0, real.shape[2], 2 * CHUNK):
        for index, group in enumerate(parent_groups(rows, cols)):
            sums = parent_sums(
                rows, cols, sides, table, pops, sources, index, group, first, 2 * CHUNK
            )
            for (r, c), (re, im) in zip(group, sums):
                real[r * cols + c, :, first : first + 2 * CHUNK] = re
                imag[r * cols + c, :, first : first + 2 * CHUNK] = im


def last_kernel(
    rows, cols, sides,
    table,
    src, interp, trig, fops, pops, real, imag, near_own, near_a,
    out,
    fine, even, odd, pat_b, child, near_b, acc,
):
    comps, fdirs = fine.shape[1:]
    fcols = 2 * cols
    par_counts = slot_counts(rows, cols, 1)
    a_right = 1 - parity("dir")
    steps = interp.shape[1] // CHUNK

    def store(at, value):
        near_b[1 - a_right, at] = value

    def beside():
        near_side(table, fops, fine, rows, cols, 3, 1 - a_right, store, PARITIES)

    def keep():
        for at in range(near_a.shape[0]):
            near_b[a_right, at] = near_a[at]

    def far(j):
        lanes = slice(j * CHUNK, (j + 1) * CHUNK)
        cos, sin = shift_rows(trig, lanes, comps)
        sources = [(starts(par_counts)[2], par_counts[2], pat_b)]
        for index, group in enumerate(parent_groups(rows, cols)):
            sums = parent_sums(rows, cols, sides, table, pops, sources, index, group, j * CHUNK, CHUNK)
            for (r, c), (re, im) in zip(group, sums):
                box = r * cols + c
                total = re + real[box, :, lanes] + times_i(im + imag[box, :, lanes], sides)
                total = total.astype(BF16).astype(F32)
                turned = pltpu.roll(total, sides, 0)
                for k in range(4):
                    at = (2 * r + k // 2) * fcols + 2 * c + k % 2
                    child[at, :, lanes] = (cos[k] * total + sin[k] * turned).astype(BF16)

    def back(j):
        lanes = slice(j * CHUNK, (j + 1) * CHUNK)
        more = lax.dot_general(
            child[:, :, lanes].reshape(-1, CHUNK), interp[:, lanes],
            (((1,), (1,)), ((), ())), preferred_element_type=F32,
        ).reshape(acc.shape)
        acc[...] = more if j == 0 else acc[...] + more

    spread, sums = aggregate_tasks(src, interp, trig, (even, odd), pat_b, halo_sizes(cols)[1], sides)
    plan = [[] for _ in range(steps + 3)]
    for j in range(steps):
        plan[j].append(spread[j])
        plan[j + 1].append(sums[j])
        plan[j + 2].append(functools.partial(far, j))
        plan[min(j + 4, steps + 2) if j + 1 < steps else steps + 2].append(functools.partial(back, j))
    plan[0] += [
        functools.partial(widen, src, fine, comps), functools.partial(zero_box, pat_b), beside, keep,
    ]
    in_steps(plan)

    scale = fdirs / interp.shape[1]
    for r in range(2 * rows):
        for c in range(fcols):
            at = r * fcols + c
            value = near_own[at] + acc[at] * scale
            if c < 2:
                value = value + near_b[0, r * 2 + c]
            if c >= fcols - 2:
                value = value + near_b[1, r * 2 + c - (fcols - 2)]
            out[r, c, 0] = value[:sides]
            out[r, c, 1] = value[sides:]


def per_device(
    fine_out, interp, child_phase, fine_ops, parent_ops, fine_src, fine_op, parent_src, parent_op
):
    frows, fcols, _, sides, fdirs = fine_out.shape
    rows, cols = frows // 2, fcols // 2
    comps = 2 * sides
    pdirs = interp.shape[1]
    assert all(size == cols for size in halo_sizes(cols)) and pdirs % (2 * CHUNK) == 0
    height = rows + sum(halo_sizes(rows))
    boxes = height * cols
    n_dir, bits = lax.axis_size("dir"), swap_bits("dir")

    own = fine_out.reshape(frows * fcols * comps, fdirs)
    outside = boxes - rows * cols
    sources, op_ids, nothing = build_tables(
        rows, cols, {2: [frows * fcols, 4 * outside, 4 * boxes, 4 * boxes], 1: [boxes] * 3}
    )
    ids = shared_ids(op_ids, rows, cols)
    ids = np.pad(ids, [(0, 0), (0, 0), (0, sources.shape[2] - ids.shape[2])])
    nothing = np.broadcast_to(nothing[[0, -1]], (len(PARITIES), 2, nothing.shape[1]))
    lists = jnp.asarray(np.concatenate([sources, op_ids, nothing, ids], axis=1))

    smem = pl.BlockSpec(memory_space=pltpu.SMEM)
    vmem = pl.BlockSpec(memory_space=pltpu.VMEM)

    def shape(*dims):
        return jax.ShapeDtypeStruct(dims, F32)

    def scratch(*dims, kind=F32):
        return pltpu.VMEM(dims, kind)

    def group_scratch(count):
        return [scratch(count + 1, comps, fdirs)] + [scratch(count, comps, CHUNK)] * 2

    def call(body, name, n_smem, outs, scratches, *args):
        return pl.pallas_call(
            functools.partial(body, rows, cols, sides),
            out_shape=outs,
            in_specs=[smem] * n_smem + [vmem] * (len(args) - n_smem),
            out_specs=[vmem] * len(outs),
            scratch_shapes=scratches,
            compiler_params=pltpu.CompilerParams(vmem_limit_bytes=LIMITS[name] << 20),
            name=name,
        )(*args)

    near = shape(frows * fcols, comps, fdirs)
    pattern = shape(boxes + 1, comps, pdirs)
    table = call(
        lists_kernel, "lists", 0, [jax.ShapeDtypeStruct((5 * rows * cols + ids.shape[1], ids.shape[2]), jnp.int32)], [],
        fine_op, parent_op, lists,
    )[0]
    first, second = halo_sizes(rows)
    assert first == rows
    edge = call(
        edge_kernel, "edge", 0,
        [jax.ShapeDtypeStruct((own.shape[0] // rows * second, fdirs), BF16)], [], own,
    )[0]
    patch_halo = exchange([own, edge], "patch")
    shards = [parent_ops[None]]
    for bit in reversed(range(bits)):
        held = jnp.concatenate(shards, axis=0)
        shards.append(lax.ppermute(held, "dir", [(i, i ^ (1 << bit)) for i in range(n_dir)]))
    near_block, trig = call(
        block_kernel, "block", 1, [near, shape(8, pdirs)], [scratch(frows * fcols + 1, comps, fdirs)],
        table, own, child_phase, fine_ops,
    )
    strip = call(
        pack_kernel, "pack", 0,
        [jax.ShapeDtypeStruct((4 * boxes * comps, fdirs), BF16)], [], own, *patch_halo, near_block,
    )[0]
    side_a, side_b = exchange([strip, strip], "dir")
    if parent_ops.shape[2] % 128:
        shards = [in_order(jnp.concatenate(shards, axis=0), "dir")]
    pat_own, near_own, pat_a, near_a = call(
        both_kernel, "both", 1, [pattern, near, pattern, shape(frows * 2, comps, fdirs)],
        [scratch(4 * outside + 1, comps, fdirs), scratch(4 * boxes + 1, comps, fdirs)] + [scratch(8 * boxes, comps, CHUNK)] * 2,
        table, strip, side_a, interp, trig, fine_ops, near_block,
    )
    part = shape(rows * cols, comps, pdirs)
    pops, real, imag = call(
        inner_kernel, "inner", 1, [shape(parent_ops.shape[0], 2, pdirs), part, part], [],
        table, pat_own, pat_a, *shards,
    )
    return call(
        last_kernel, "last", 1, [jax.ShapeDtypeStruct(fine_out.shape, F32)],
        group_scratch(4 * boxes) + [
            scratch(boxes + 1, comps, pdirs),
            scratch(frows * fcols, comps, pdirs, kind=BF16),
            scratch(2, frows * 2, comps, fdirs),
            scratch(frows * fcols, comps, fdirs),
        ],
        table, side_b, interp, trig, fine_ops, pops, real, imag, near_own, near_a,
    )[0]


def solution(mesh):
    in_specs = (
        P("patch", "dir", None, None, None),
        P(),
        P(),
        P(),
        P(None, None, "dir"),
        P("patch", None, None),
        P("patch", None, None),
        P("patch", None, None),
        P("patch", None, None),
    )
    out_specs = P("patch", "dir", None, None, None)
    return jax.shard_map(
        per_device, mesh=mesh, in_specs=in_specs, out_specs=out_specs, check_vma=False
    )
```

```python
import functools

import jax
import jax.numpy as jnp
import numpy as np
from jax import lax
from jax.experimental import pallas as pl
from jax.experimental.pallas import tpu as pltpu
from jax.sharding import PartitionSpec as P

CHUNK = 512
COSTS = {"hold2": 0.5, "hold3": 0.5, "edge": 0.5}
PIECE = 256
LIMITS = {"block": 8, "pack": 4, "edge": 4, "lists": 4, "both": 20, "inner": 12, "last": 24}
F32, BF16 = jnp.float32, jnp.bfloat16


def offset_pairs():
    return [(dr, dc) for dr in range(-3, 4) for dc in range(-3, 4) if max(abs(dr), abs(dc)) > 1]


def class_offsets(row_odd, col_odd):
    return [
        (op_id, dr, dc)
        for op_id, (dr, dc) in enumerate(offset_pairs())
        if -2 <= dr + row_odd <= 3 and -2 <= dc + col_odd <= 3
    ]


def halo_sizes(count):
    return (3, 2) if count % 2 else (2, 2)


def stored_at(rel, count, odd):
    first, second = halo_sizes(count)
    if 0 <= rel < count:
        return rel
    if rel < 0:
        return count + first + rel if odd else count + first + second + rel
    return rel if not odd else rel + first


def place(row, col, rows, cols, row_odd, col_odd, scale):
    at_r = stored_at(row // scale, rows, row_odd) * scale + row % scale
    at_c = stored_at(col // scale, cols, col_odd) * scale + col % scale
    for group, width in enumerate((cols, *halo_sizes(cols))):
        if at_c < width * scale:
            return group, at_r * width * scale + at_c
        at_c -= width * scale


def fine_slots(row, col, rows, cols, row_odd, col_odd):
    inside, found = 4 * rows * cols, ([], [], [], [])
    for op_id, dr, dc in class_offsets(row % 2, col % 2):
        group, index = place(row + dr, col + dc, rows, cols, row_odd, col_odd, 2)
        if group:
            found[group + 1].append((op_id, index))
        elif index >= inside:
            found[0].append((op_id, None))
            found[1].append((op_id, index - inside))
        else:
            found[0].append((op_id, index))
    return found


def parent_slots(row, col, rows, cols, row_odd, col_odd):
    found = ([], [], [])
    for op_id, dr, dc in class_offsets((row + row_odd * rows) % 2, (col + col_odd * cols) % 2):
        group, index = place(row + dr, col + dc, rows, cols, row_odd, col_odd, 1)
        found[group].append((op_id, index))
    return found


PARITIES = [(a, b) for a in range(2) for b in range(2)]


def slot_counts(rows, cols, scale):
    slots = fine_slots if scale == 2 else parent_slots
    lists = [
        [len(found) for found in slots(r, c, rows, cols, *odd)]
        for odd in PARITIES for r in range(rows * scale) for c in range(cols * scale)
    ]
    most = [max(column) for column in zip(*lists)]
    return most[:-2] + [max(most[-2:])] * 2


def starts(counts):
    return [sum(counts[:i]) for i in range(len(counts))]


def build_tables(rows, cols, zeros):
    counts = {scale: slot_counts(rows, cols, scale) for scale in (2, 1)}
    width = max(sum(c) for c in counts.values())
    sources, op_ids, nothing = [], [], []
    for odd in PARITIES:
        src_rows, id_rows, none_rows = [], [], []
        for scale, slots in ((2, fine_slots), (1, parent_slots)):
            for r in range(rows * scale):
                for c in range(cols * scale):
                    src_row, id_row, none_row = [], [], []
                    for size, found, zero in zip(counts[scale], slots(r, c, rows, cols, *odd), zeros[scale]):
                        found = found + [(0, None)] * (size - len(found))
                        src_row += [zero if at is None else at for _, at in found]
                        id_row += [o for o, _ in found]
                        none_row += [zero] * size
                    pad = [0] * (width - len(src_row))
                    src_rows.append(src_row + pad)
                    id_rows.append(id_row + pad)
                    none_rows.append(none_row + pad)
        sources.append(src_rows)
        op_ids.append(id_rows)
        nothing = none_rows
    return np.array(sources, np.int32), np.array(op_ids, np.int32), np.array(nothing, np.int32)


def shared_ids(op_ids, rows, cols):
    fine, par = slot_counts(rows, cols, 2), slot_counts(rows, cols, 1)
    width = max(2 * fine[2], sum(par))
    found = []
    for which, (_, dir_odd) in enumerate(PARITIES):
        entries = []
        for a in range(2):
            for c in range(2):
                entry = []
                for group, right in ((2, 1 - dir_odd), (3, dir_odd)):
                    box = a * 2 * cols + right * (2 * cols - 2) + c
                    at = starts(fine)[group]
                    entry += list(op_ids[which, box, at : at + fine[group]])
                entries.append(entry)
        for c in range(cols):
            for start in range(2):
                entries.append(list(op_ids[which, 4 * rows * cols + start * cols + c, : sum(par)]))
        found.append([entry + [0] * (width - len(entry)) for entry in entries])
    return np.array(found, np.int32)


def parity(axis):
    return lax.rem(lax.axis_index(axis), 2)


def parities():
    return parity("patch") * 2 + parity("dir")


def pairs(count, first):
    if first:
        return [(i, i ^ 1) for i in range(count) if (i ^ 1) < count]
    found = []
    for i in range(1, count - 1, 2):
        found += [(i, i + 1), (i + 1, i)]
    return found


def exchange(blocks, axis):
    n = lax.axis_size(axis)
    return [lax.ppermute(block, axis, pairs(n, first)) for block, first in zip(blocks, (True, False))]


def swap_bits(axis):
    return lax.axis_size(axis).bit_length() - 1


def shard_order(axis):
    bits = swap_bits(axis)
    return [int(format(e, "0%db" % bits)[::-1], 2) if bits else 0 for e in range(lax.axis_size(axis))]


def in_order(block, axis):
    n = lax.axis_size(axis)
    at = jnp.asarray(np.array(shard_order(axis), np.int32))[jnp.arange(n, dtype=jnp.int32) ^ lax.axis_index(axis)]
    block = jnp.take(block, at, axis=0)
    return block.transpose(1, 2, 0, 3).reshape(1, block.shape[1], 2, n * block.shape[3])


def times_i(v, sides):
    sign = jnp.where(lax.broadcasted_iota(jnp.int32, (2 * sides, 1), 0) < sides, -1.0, 1.0)
    return sign.astype(F32) * pltpu.roll(v, sides, 0)


def row_of(ref, lead, part, lane, width, comps):
    return jnp.broadcast_to(ref[(*lead, slice(part, part + 1), pl.ds(lane, width))], (comps, width))


def add_slots(sums, coefs, pieces):
    real, imag = coefs
    for m, piece in enumerate(pieces):
        add = [real * piece, imag * piece]
        sums[m] = add if sums[m] is None else [a + b for a, b in zip(sums[m], add)]


def widen(src, fine, comps):
    count = src.shape[0] // comps
    fine[:count] = src[...].astype(F32).reshape(count, comps, src.shape[1])
    fine[count] = jnp.zeros(fine.shape[1:], F32)


def spread_chunk(src, interp, j, buffer, comps):
    lanes = slice(j * CHUNK, (j + 1) * CHUNK)
    out = jnp.dot(src[...], interp[:, lanes], preferred_element_type=F32)
    buffer[...] = out.reshape(-1, comps, CHUNK)


def in_steps(steps):
    for tasks in steps:
        for task in tasks:
            task()


def shift_rows(trig, lanes, comps):
    width = lanes.stop - lanes.start
    sign = jnp.where(lax.broadcasted_iota(jnp.int32, (comps, 1), 0) < comps // 2, 1.0, -1.0).astype(F32)
    rows = [jnp.broadcast_to(trig[k : k + 1, lanes], (comps, width)) for k in range(8)]
    return rows[:4], [sign * row for row in rows[4:]]


def aggregate_chunk(buffer, trig, j, pattern, width, sides):
    comps = 2 * sides
    for at in range(0, CHUNK, PIECE):
        lanes = slice(j * CHUNK + at, j * CHUNK + at + PIECE)
        shift = shift_rows(trig, lanes, comps)
        for q in range(buffer.shape[0] // 4):
            r, c = divmod(q, width)
            total = [None, None]
            for k in range(4):
                piece = buffer[(2 * r + k // 2) * (2 * width) + 2 * c + k % 2, :, at : at + PIECE]
                for i in range(2):
                    add = shift[i][k] * piece
                    total[i] = add if k == 0 else total[i] + add
            whole = total[0] + pltpu.roll(total[1], sides, 0)
            pattern[q, :, lanes] = whole.astype(BF16).astype(F32)


def aggregate_tasks(src, interp, trig, buffers, pattern, width, sides):
    steps = range(interp.shape[1] // CHUNK)
    spread = [
        functools.partial(spread_chunk, src, interp, j, buffers[j % 2], 2 * sides) for j in steps
    ]
    sums = [
        functools.partial(aggregate_chunk, buffers[j % 2], trig, j, pattern, width, sides) for j in steps
    ]
    return spread, sums


def dealt(items, j, steps):
    return items[len(items) * j // steps : len(items) * (j + 1) // steps]


def zero_box(pattern):
    pattern[pattern.shape[0] - 1] = jnp.zeros(pattern.shape[1:], F32)


def near_sums(table, fops, fine, group, base, op_ids):
    comps, fdirs = fine.shape[1:]
    sums = [None] * len(group)
    for t, op_id in enumerate(op_ids, base):
        coefs = [row_of(fops, (op_id,), i, 0, fdirs, comps) for i in range(2)]
        add_slots(sums, coefs, [fine[table[box, t]] for box in group])
    return [real + times_i(imag, comps // 2) for real, imag in sums]


def near_side(table, fops, fine, rows, cols, group, right, store, classes):
    counts = slot_counts(rows, cols, 2)
    base, count = starts(counts)[group], counts[group]
    first_col = right * (2 * cols - 2)
    for a, c in classes:
        boxes = [(2 * r + a) * (2 * cols) + first_col + c for r in range(rows)]
        op_ids = [table[5 * rows * cols + 2 * a + c, (group - 2) * count + t] for t in range(count)]
        for r, value in enumerate(near_sums(table, fops, fine, boxes, base, op_ids)):
            store((2 * r + a) * 2 + c, value)


def block_kernel(rows, cols, sides, table, src, phase, fops, near, trig, fine):
    half = phase.shape[1] // 2
    both = jnp.concatenate([phase[:, :half], phase[:, half:]], axis=0)
    for first, wave in ((0, jnp.cos(both)), (4, jnp.sin(both))):
        trig[first : first + 4, :half] = wave[:4]
        trig[first : first + 4, half:] = wave[4:]
    widen(src, fine, 2 * sides)
    for a in range(2):
        for c in range(2 * cols):
            op_ids = [o for o, _ in fine_slots(a, c, rows, cols, 0, 0)[0]]
            group = [(2 * r + a) * (2 * cols) + c for r in range(rows)]
            for box, value in zip(group, near_sums(table, fops, fine, group, 0, op_ids)):
                near[box] = value


def hold_kernel(rows, cols, sides, *refs):
    *shards, out = refs
    at = 0
    for ref in shards:
        out[at : at + ref.shape[0]] = ref[...]
        at += ref.shape[0]


def lists_kernel(rows, cols, sides, fine_op, par_op, lists, table):
    which = parities()
    at, boxes = 0, 5 * rows * cols
    table[boxes:] = lists[which, 2 * boxes + 2 :]
    for op, scale, none in ((fine_op, 2, 2 * boxes), (par_op, 1, 2 * boxes + 1)):
        across = cols * scale
        first = pl.multiple_of(lax.axis_index("dir") * across, across)
        for r in range(rows * scale):
            mine = op[r, pl.ds(first, across), :]
            wanted = lists[which, boxes + at : boxes + at + across]
            found = mine[:, 0:1] == wanted
            for slot in range(1, op.shape[2]):
                found = found | (mine[:, slot : slot + 1] == wanted)
            zero = jnp.broadcast_to(lists[which, none : none + 1], wanted.shape)
            table[at : at + across] = jnp.where(found, lists[which, at : at + across], zero)
            at += across


def edge_kernel(rows, cols, sides, own, edge):
    size = halo_sizes(rows)[1]
    unit = own.shape[0] // rows
    at = pl.multiple_of(parity("patch") * ((rows - size) * unit), unit)
    edge[...] = own[pl.ds(at, size * unit)]


def pack_kernel(rows, cols, sides, own, first, second, after, strip):
    at = 0
    for ref in (own, first, second):
        strip[at : at + ref.shape[0]] = ref[...]
        at += ref.shape[0]


def both_kernel(
    rows, cols, sides, table, strip, side_a, interp, trig, fops, near_block,
    pat_own, near, pat_a, near_a, fine, fine_a, even, odd,
):
    base = starts(slot_counts(rows, cols, 2))[1]
    inside = near.shape[0] * 2 * sides
    buffers = (even, odd)
    steps = interp.shape[1] // CHUNK

    def halo(boxes):
        for box in boxes:
            op_ids = [o for o, _ in fine_slots(*divmod(box, 2 * cols), rows, cols, 0, 0)[1]]
            more = near_sums(table, fops, fine, [box], base, op_ids)[0] if op_ids else 0.0
            near[box] = near_block[box] + more

    def store(at, value):
        near_a[at] = value

    def beside(classes):
        near_side(table, fops, fine_a, rows, cols, 2, 1 - parity("dir"), store, classes)

    widen(strip.at[pl.ds(inside, strip.shape[0] - inside)], fine, 2 * sides)
    widen(side_a, fine_a, 2 * sides)
    zero_box(pat_own)
    zero_box(pat_a)
    boxes = strip.shape[0] // (2 * sides)
    whole = jnp.concatenate([strip[...], side_a[...]], axis=0)
    for j in range(steps + 1):
        if j < steps:
            spread_chunk(whole, interp, j, buffers[j % 2], 2 * sides)
        if j < 2:
            beside(PARITIES[2 * j : 2 * j + 2])
        if j in (2, 3):
            halo(dealt(range(near.shape[0]), j - 2, 2))
        if j:
            buffer = buffers[(j - 1) % 2]
            aggregate_chunk(buffer.at[pl.ds(0, boxes)], trig, j - 1, pat_own, cols, sides)
            aggregate_chunk(buffer.at[pl.ds(boxes, boxes)], trig, j - 1, pat_a, halo_sizes(cols)[0], sides)


def parent_groups(rows, cols):
    return [[(r, c) for r in range(start, rows, 2)] for c in range(cols) for start in range(2)]


def parent_sums(rows, cols, sides, table, pops, sources, index, group, first, width):
    comps = 2 * sides
    rows_at = [4 * rows * cols + r * cols + c for r, c in group]
    sums = [None] * len(group)
    for base, count, ref in sources:
        for t in range(base, base + count):
            op_id = table[5 * rows * cols + 4 + index, t]
            coefs = [row_of(pops, (op_id,), i, first, width, comps) for i in range(2)]
            add_slots(sums, coefs, [ref[table[row, t], :, first : first + width] for row in rows_at])
    return sums


def inner_kernel(rows, cols, sides, table, pat_own, pat_a, *refs):
    *shards, pops, real, imag = refs
    at = 0
    for ref in shards:
        held = ref.shape[3]
        for k in range(ref.shape[0]):
            lane = pl.multiple_of((shard_order("dir")[at] ^ lax.axis_index("dir")) * held, held) if held < pops.shape[2] else 0
            pops[:, :, pl.ds(lane, held)] = ref[k]
            at += 1
    counts = slot_counts(rows, cols, 1)
    at = starts(counts)
    sources = [(at[0], counts[0], pat_own), (at[1], counts[1], pat_a)]
    for first in range(0, real.shape[2], 2 * CHUNK):
        for index, group in enumerate(parent_groups(rows, cols)):
            sums = parent_sums(
                rows, cols, sides, table, pops, sources, index, group, first, 2 * CHUNK
            )
            for (r, c), (re, im) in zip(group, sums):
                real[r * cols + c, :, first : first + 2 * CHUNK] = re
                imag[r * cols + c, :, first : first + 2 * CHUNK] = im


def last_kernel(
    rows, cols, sides,
    table,
    src, interp, trig, fops, pops, real, imag, near_own, near_a,
    out,
    fine, even, odd, pat_b, child, near_b, acc,
):
    comps, fdirs = fine.shape[1:]
    fcols = 2 * cols
    par_counts = slot_counts(rows, cols, 1)
    a_right = 1 - parity("dir")
    steps = interp.shape[1] // CHUNK

    def store(at, value):
        near_b[1 - a_right, at] = value

    def beside():
        near_side(table, fops, fine, rows, cols, 3, 1 - a_right, store, PARITIES)

    def keep():
        for at in range(near_a.shape[0]):
            near_b[a_right, at] = near_a[at]

    def far(j):
        lanes = slice(j * CHUNK, (j + 1) * CHUNK)
        cos, sin = shift_rows(trig, lanes, comps)
        sources = [(starts(par_counts)[2], par_counts[2], pat_b)]
        for index, group in enumerate(parent_groups(rows, cols)):
            sums = parent_sums(rows, cols, sides, table, pops, sources, index, group, j * CHUNK, CHUNK)
            for (r, c), (re, im) in zip(group, sums):
                box = r * cols + c
                total = re + real[box, :, lanes] + times_i(im + imag[box, :, lanes], sides)
                total = total.astype(BF16).astype(F32)
                turned = pltpu.roll(total, sides, 0)
                for k in range(4):
                    at = (2 * r + k // 2) * fcols + 2 * c + k % 2
                    child[at, :, lanes] = (cos[k] * total + sin[k] * turned).astype(BF16)

    def back(j):
        lanes = slice(j * CHUNK, (j + 1) * CHUNK)
        more = lax.dot_general(
            child[:, :, lanes].reshape(-1, CHUNK), interp[:, lanes],
            (((1,), (1,)), ((), ())), preferred_element_type=F32,
        ).reshape(acc.shape)
        acc[...] = more if j == 0 else acc[...] + more

    spread, sums = aggregate_tasks(src, interp, trig, (even, odd), pat_b, halo_sizes(cols)[1], sides)
    plan = [[] for _ in range(steps + 3)]
    for j in range(steps):
        plan[j].append(spread[j])
        plan[j + 1].append(sums[j])
        plan[j + 2].append(functools.partial(far, j))
        plan[min(j + 4, steps + 2) if j + 1 < steps else steps + 2].append(functools.partial(back, j))
    plan[0] += [
        functools.partial(widen, src, fine, comps), functools.partial(zero_box, pat_b), beside, keep,
    ]
    in_steps(plan)

    scale = fdirs / interp.shape[1]
    for r in range(2 * rows):
        for c in range(fcols):
            at = r * fcols + c
            value = near_own[at] + acc[at] * scale
            if c < 2:
                value = value + near_b[0, r * 2 + c]
            if c >= fcols - 2:
                value = value + near_b[1, r * 2 + c - (fcols - 2)]
            out[r, c, 0] = value[:sides]
            out[r, c, 1] = value[sides:]


def per_device(
    fine_out, interp, child_phase, fine_ops, parent_ops, fine_src, fine_op, parent_src, parent_op
):
    frows, fcols, _, sides, fdirs = fine_out.shape
    rows, cols = frows // 2, fcols // 2
    comps = 2 * sides
    pdirs = interp.shape[1]
    assert all(size == cols for size in halo_sizes(cols)) and pdirs % (2 * CHUNK) == 0
    height = rows + sum(halo_sizes(rows))
    boxes = height * cols
    n_dir, bits = lax.axis_size("dir"), swap_bits("dir")

    own = fine_out.reshape(frows * fcols * comps, fdirs)
    outside = boxes - rows * cols
    sources, op_ids, nothing = build_tables(
        rows, cols, {2: [frows * fcols, 4 * outside, 4 * boxes, 4 * boxes], 1: [boxes] * 3}
    )
    ids = shared_ids(op_ids, rows, cols)
    ids = np.pad(ids, [(0, 0), (0, 0), (0, sources.shape[2] - ids.shape[2])])
    nothing = np.broadcast_to(nothing[[0, -1]], (len(PARITIES), 2, nothing.shape[1]))
    lists = jnp.asarray(np.concatenate([sources, op_ids, nothing, ids], axis=1))

    smem = pl.BlockSpec(memory_space=pltpu.SMEM)
    vmem = pl.BlockSpec(memory_space=pltpu.VMEM)

    def shape(*dims):
        return jax.ShapeDtypeStruct(dims, F32)

    def scratch(*dims, kind=F32):
        return pltpu.VMEM(dims, kind)

    def group_scratch(count):
        return [scratch(count + 1, comps, fdirs)] + [scratch(count, comps, CHUNK)] * 2

    def call(body, name, n_smem, outs, scratches, *args):
        return pl.pallas_call(
            functools.partial(body, rows, cols, sides),
            out_shape=outs,
            in_specs=[smem] * n_smem + [vmem] * (len(args) - n_smem),
            out_specs=[vmem] * len(outs),
            scratch_shapes=scratches,
            compiler_params=pltpu.CompilerParams(vmem_limit_bytes=LIMITS.get(name, 4) << 20),
            cost_estimate=pl.CostEstimate(flops=int(COSTS.get(name, 0) * 10**9), bytes_accessed=0, transcendentals=0),
            name=name,
        )(*args)

    near = shape(frows * fcols, comps, fdirs)
    pattern = shape(boxes + 1, comps, pdirs)
    table = call(
        lists_kernel, "lists", 0, [jax.ShapeDtypeStruct((5 * rows * cols + ids.shape[1], ids.shape[2]), jnp.int32)], [],
        fine_op, parent_op, lists,
    )[0]
    first, second = halo_sizes(rows)
    assert first == rows
    edge = call(
        edge_kernel, "edge", 0,
        [jax.ShapeDtypeStruct((own.shape[0] // rows * second, fdirs), BF16)], [], own,
    )[0]
    patch_halo = exchange([own, edge], "patch")
    shards = [parent_ops[None]]
    for bit in reversed(range(bits)):
        held = shards[0]
        if len(shards) > 1:
            count = sum(part.shape[0] for part in shards)
            held = call(hold_kernel, "hold%d" % len(shards), 0, [shape(count, *parent_ops.shape)], [], *shards)[0]
        shards.append(lax.ppermute(held, "dir", [(i, i ^ (1 << bit)) for i in range(n_dir)]))
    near_block, trig = call(
        block_kernel, "block", 1, [near, shape(8, pdirs)], [scratch(frows * fcols + 1, comps, fdirs)],
        table, own, child_phase, fine_ops,
    )
    strip = call(
        pack_kernel, "pack", 0,
        [jax.ShapeDtypeStruct((4 * boxes * comps, fdirs), BF16)], [], own, *patch_halo, near_block,
    )[0]
    side_a, side_b = exchange([strip, strip], "dir")
    if parent_ops.shape[2] % 128:
        shards = [in_order(jnp.concatenate(shards, axis=0), "dir")]
    pat_own, near_own, pat_a, near_a = call(
        both_kernel, "both", 1, [pattern, near, pattern, shape(frows * 2, comps, fdirs)],
        [scratch(4 * outside + 1, comps, fdirs), scratch(4 * boxes + 1, comps, fdirs)] + [scratch(8 * boxes, comps, CHUNK)] * 2,
        table, strip, side_a, interp, trig, fine_ops, near_block,
    )
    part = shape(rows * cols, comps, pdirs)
    pops, real, imag = call(
        inner_kernel, "inner", 1, [shape(parent_ops.shape[0], 2, pdirs), part, part], [],
        table, pat_own, pat_a, *shards,
    )
    return call(
        last_kernel, "last", 1, [jax.ShapeDtypeStruct(fine_out.shape, F32)],
        group_scratch(4 * boxes) + [
            scratch(boxes + 1, comps, pdirs),
            scratch(frows * fcols, comps, pdirs, kind=BF16),
            scratch(2, frows * 2, comps, fdirs),
            scratch(frows * fcols, comps, fdirs),
        ],
        table, side_b, interp, trig, fine_ops, pops, real, imag, near_own, near_a,
    )[0]


def solution(mesh):
    in_specs = (
        P("patch", "dir", None, None, None),
        P(),
        P(),
        P(),
        P(None, None, "dir"),
        P("patch", None, None),
        P("patch", None, None),
        P("patch", None, None),
        P("patch", None, None),
    )
    out_specs = P("patch", "dir", None, None, None)
    return jax.shard_map(
        per_device, mesh=mesh, in_specs=in_specs, out_specs=out_specs, check_vma=False
    )
```

```python
import functools

import jax
import jax.numpy as jnp
import numpy as np
from jax import lax
from jax.experimental import pallas as pl
from jax.experimental.pallas import tpu as pltpu
from jax.sharding import PartitionSpec as P

CHUNK = 512
COSTS = {"hold2": 0.5, "hold3": 0.5, "edge": 0.5}
PIECE = 256
TILE = 8
LIMITS = {"block": 8, "pack": 4, "edge": 4, "lists": 4, "both": 20, "inner": 12, "last": 24}
F32, BF16 = jnp.float32, jnp.bfloat16


def offset_pairs():
    return [(dr, dc) for dr in range(-3, 4) for dc in range(-3, 4) if max(abs(dr), abs(dc)) > 1]


def class_offsets(row_odd, col_odd):
    return [
        (op_id, dr, dc)
        for op_id, (dr, dc) in enumerate(offset_pairs())
        if -2 <= dr + row_odd <= 3 and -2 <= dc + col_odd <= 3
    ]


def halo_sizes(count):
    return (3, 2) if count % 2 else (2, 2)


def stored_at(rel, count, odd):
    first, second = halo_sizes(count)
    if 0 <= rel < count:
        return rel
    if rel < 0:
        return count + first + rel if odd else count + first + second + rel
    return rel if not odd else rel + first


def place(row, col, rows, cols, row_odd, col_odd, scale):
    at_r = stored_at(row // scale, rows, row_odd) * scale + row % scale
    at_c = stored_at(col // scale, cols, col_odd) * scale + col % scale
    for group, width in enumerate((cols, *halo_sizes(cols))):
        if at_c < width * scale:
            return group, at_r * width * scale + at_c
        at_c -= width * scale


def fine_slots(row, col, rows, cols, row_odd, col_odd):
    inside, found = 4 * rows * cols, ([], [], [], [])
    for op_id, dr, dc in class_offsets(row % 2, col % 2):
        group, index = place(row + dr, col + dc, rows, cols, row_odd, col_odd, 2)
        if group:
            found[group + 1].append((op_id, index))
        elif index >= inside:
            found[0].append((op_id, None))
            found[1].append((op_id, index - inside))
        else:
            found[0].append((op_id, index))
    return found


def parent_slots(row, col, rows, cols, row_odd, col_odd):
    found = ([], [], [])
    for op_id, dr, dc in class_offsets((row + row_odd * rows) % 2, (col + col_odd * cols) % 2):
        group, index = place(row + dr, col + dc, rows, cols, row_odd, col_odd, 1)
        found[group].append((op_id, index))
    return found


PARITIES = [(a, b) for a in range(2) for b in range(2)]


def slot_counts(rows, cols, scale):
    slots = fine_slots if scale == 2 else parent_slots
    lists = [
        [len(found) for found in slots(r, c, rows, cols, *odd)]
        for odd in PARITIES for r in range(rows * scale) for c in range(cols * scale)
    ]
    most = [max(column) for column in zip(*lists)]
    return most[:-2] + [max(most[-2:])] * 2


def starts(counts):
    return [sum(counts[:i]) for i in range(len(counts))]


def build_tables(rows, cols, zeros):
    counts = {scale: slot_counts(rows, cols, scale) for scale in (2, 1)}
    width = max(sum(c) for c in counts.values())
    sources, op_ids, nothing = [], [], []
    for odd in PARITIES:
        src_rows, id_rows, none_rows = [], [], []
        for scale, slots in ((2, fine_slots), (1, parent_slots)):
            for r in range(rows * scale):
                for c in range(cols * scale):
                    src_row, id_row, none_row = [], [], []
                    for size, found, zero in zip(counts[scale], slots(r, c, rows, cols, *odd), zeros[scale]):
                        found = found + [(0, None)] * (size - len(found))
                        src_row += [zero if at is None else at for _, at in found]
                        id_row += [o for o, _ in found]
                        none_row += [zero] * size
                    pad = [0] * (width - len(src_row))
                    src_rows.append(src_row + pad)
                    id_rows.append(id_row + pad)
                    none_rows.append(none_row + pad)
        sources.append(src_rows)
        op_ids.append(id_rows)
        nothing = none_rows
    return np.array(sources, np.int32), np.array(op_ids, np.int32), np.array(nothing, np.int32)


def shared_ids(op_ids, rows, cols):
    fine, par = slot_counts(rows, cols, 2), slot_counts(rows, cols, 1)
    width = max(2 * fine[2], sum(par))
    found = []
    for which, (_, dir_odd) in enumerate(PARITIES):
        entries = []
        for a in range(2):
            for c in range(2):
                entry = []
                for group, right in ((2, 1 - dir_odd), (3, dir_odd)):
                    box = a * 2 * cols + right * (2 * cols - 2) + c
                    at = starts(fine)[group]
                    entry += list(op_ids[which, box, at : at + fine[group]])
                entries.append(entry)
        for c in range(cols):
            for start in range(2):
                entries.append(list(op_ids[which, 4 * rows * cols + start * cols + c, : sum(par)]))
        found.append([entry + [0] * (width - len(entry)) for entry in entries])
    return np.array(found, np.int32)


def parity(axis):
    return lax.rem(lax.axis_index(axis), 2)


def parities():
    return parity("patch") * 2 + parity("dir")


def pairs(count, first):
    if first:
        return [(i, i ^ 1) for i in range(count) if (i ^ 1) < count]
    found = []
    for i in range(1, count - 1, 2):
        found += [(i, i + 1), (i + 1, i)]
    return found


def exchange(blocks, axis):
    n = lax.axis_size(axis)
    return [lax.ppermute(block, axis, pairs(n, first)) for block, first in zip(blocks, (True, False))]


def swap_bits(axis):
    return lax.axis_size(axis).bit_length() - 1


def shard_order(axis):
    bits = swap_bits(axis)
    return [int(format(e, "0%db" % bits)[::-1], 2) if bits else 0 for e in range(lax.axis_size(axis))]


def in_order(block, axis):
    n = lax.axis_size(axis)
    at = jnp.asarray(np.array(shard_order(axis), np.int32))[jnp.arange(n, dtype=jnp.int32) ^ lax.axis_index(axis)]
    block = jnp.take(block, at, axis=0)
    return block.transpose(1, 2, 0, 3).reshape(1, block.shape[1], 2, n * block.shape[3])


def times_i(v, sides):
    sign = jnp.where(lax.broadcasted_iota(jnp.int32, (2 * sides, 1), 0) < sides, -1.0, 1.0)
    return sign.astype(F32) * pltpu.roll(v, sides, 0)


def row_of(ref, lead, part, lane, width, comps):
    return jnp.broadcast_to(ref[(*lead, slice(part, part + 1), pl.ds(lane, width))], (comps, width))


def add_slots(sums, coefs, pieces):
    real, imag = coefs
    for m, piece in enumerate(pieces):
        add = [real * piece, imag * piece]
        sums[m] = add if sums[m] is None else [a + b for a, b in zip(sums[m], add)]


def widen(src, fine, comps):
    count = src.shape[0] // comps
    fine[:count] = src[...].astype(F32).reshape(count, comps, src.shape[1])
    fine[count] = jnp.zeros(fine.shape[1:], F32)


def spread_chunk(src, interp, j, buffer, comps):
    lanes = slice(j * CHUNK, (j + 1) * CHUNK)
    out = jnp.dot(src[...], interp[:, lanes], preferred_element_type=F32)
    buffer[...] = out.reshape(-1, comps, CHUNK)


def in_steps(steps):
    for tasks in steps:
        for task in tasks:
            task()


def shift_rows(trig, lanes, comps):
    width = lanes.stop - lanes.start
    sign = jnp.where(lax.broadcasted_iota(jnp.int32, (comps, 1), 0) < comps // 2, 1.0, -1.0).astype(F32)
    rows = [jnp.broadcast_to(trig[k : k + 1, lanes], (comps, width)) for k in range(8)]
    return rows[:4], [sign * row for row in rows[4:]]


def aggregate_chunk(buffer, trig, j, pattern, width, sides):
    comps = 2 * sides
    for at in range(0, CHUNK, PIECE):
        lanes = slice(j * CHUNK + at, j * CHUNK + at + PIECE)
        shift = shift_rows(trig, lanes, comps)
        for q in range(buffer.shape[0] // 4):
            r, c = divmod(q, width)
            total = [None, None]
            for k in range(4):
                piece = buffer[(2 * r + k // 2) * (2 * width) + 2 * c + k % 2, :, at : at + PIECE]
                for i in range(2):
                    add = shift[i][k] * piece
                    total[i] = add if k == 0 else total[i] + add
            whole = total[0] + pltpu.roll(total[1], sides, 0)
            pattern[q, :, lanes] = whole.astype(BF16).astype(F32)


def aggregate_tasks(src, interp, trig, buffers, pattern, width, sides):
    steps = range(interp.shape[1] // CHUNK)
    spread = [
        functools.partial(spread_chunk, src, interp, j, buffers[j % 2], 2 * sides) for j in steps
    ]
    sums = [
        functools.partial(aggregate_chunk, buffers[j % 2], trig, j, pattern, width, sides) for j in steps
    ]
    return spread, sums


def dealt(items, j, steps):
    return items[len(items) * j // steps : len(items) * (j + 1) // steps]


def zero_box(pattern):
    pattern[pattern.shape[0] - 1] = jnp.zeros(pattern.shape[1:], F32)


def near_sums(table, fops, fine, group, base, op_ids):
    comps, fdirs = fine.shape[1:]
    sums = [None] * len(group)
    for t, op_id in enumerate(op_ids, base):
        coefs = [row_of(fops, (op_id,), i, 0, fdirs, comps) for i in range(2)]
        add_slots(sums, coefs, [fine[table[box, t]] for box in group])
    return [real + times_i(imag, comps // 2) for real, imag in sums]


def near_side(table, fops, fine, rows, cols, group, right, store, classes):
    counts = slot_counts(rows, cols, 2)
    base, count = starts(counts)[group], counts[group]
    first_col = right * (2 * cols - 2)
    for a, c in classes:
        boxes = [(2 * r + a) * (2 * cols) + first_col + c for r in range(rows)]
        op_ids = [table[5 * rows * cols + 2 * a + c, (group - 2) * count + t] for t in range(count)]
        for r, value in enumerate(near_sums(table, fops, fine, boxes, base, op_ids)):
            store((2 * r + a) * 2 + c, value)


def block_kernel(rows, cols, sides, table, src, phase, fops, near, trig, fine):
    half = phase.shape[1] // 2
    both = jnp.concatenate([phase[:, :half], phase[:, half:]], axis=0)
    for first, wave in ((0, jnp.cos(both)), (4, jnp.sin(both))):
        trig[first : first + 4, :half] = wave[:4]
        trig[first : first + 4, half:] = wave[4:]
    widen(src, fine, 2 * sides)
    for a in range(2):
        for c in range(2 * cols):
            op_ids = [o for o, _ in fine_slots(a, c, rows, cols, 0, 0)[0]]
            group = [(2 * r + a) * (2 * cols) + c for r in range(rows)]
            for box, value in zip(group, near_sums(table, fops, fine, group, 0, op_ids)):
                near[box] = value


def hold_kernel(rows, cols, sides, *refs):
    *shards, out = refs
    at = 0
    for ref in shards:
        out[at : at + ref.shape[0]] = ref[...]
        at += ref.shape[0]


def lists_kernel(rows, cols, sides, fine_op, par_op, lists, table):
    which = parities()
    at, boxes = 0, 5 * rows * cols
    table[boxes:] = lists[which, 2 * boxes + 2 :]
    for op, scale, none in ((fine_op, 2, 2 * boxes), (par_op, 1, 2 * boxes + 1)):
        across = cols * scale
        assert TILE % across == 0 and op.shape[1] % TILE == 0
        place = lax.axis_index("dir") * across
        first = pl.multiple_of(place // TILE * TILE, TILE)
        for r in range(rows * scale):
            tile = op[r, pl.ds(first, TILE), :]
            mine = tile[:across]
            for skip in range(across, TILE, across):
                mine = jnp.where(lax.rem(place, TILE) == skip, tile[skip : skip + across], mine)
            wanted = lists[which, boxes + at : boxes + at + across]
            found = mine[:, 0:1] == wanted
            for slot in range(1, op.shape[2]):
                found = found | (mine[:, slot : slot + 1] == wanted)
            zero = jnp.broadcast_to(lists[which, none : none + 1], wanted.shape)
            table[at : at + across] = jnp.where(found, lists[which, at : at + across], zero)
            at += across


def edge_kernel(rows, cols, sides, own, edge):
    size = halo_sizes(rows)[1]
    unit = own.shape[0] // rows
    at = pl.multiple_of(parity("patch") * ((rows - size) * unit), unit)
    edge[...] = own[pl.ds(at, size * unit)]


def pack_kernel(rows, cols, sides, own, first, second, after, strip):
    at = 0
    for ref in (own, first, second):
        strip[at : at + ref.shape[0]] = ref[...]
        at += ref.shape[0]


def both_kernel(
    rows, cols, sides, table, strip, side_a, interp, trig, fops, near_block,
    pat_own, near, pat_a, near_a, fine, fine_a, even, odd,
):
    base = starts(slot_counts(rows, cols, 2))[1]
    inside = near.shape[0] * 2 * sides
    buffers = (even, odd)
    steps = interp.shape[1] // CHUNK

    def halo(boxes):
        for box in boxes:
            op_ids = [o for o, _ in fine_slots(*divmod(box, 2 * cols), rows, cols, 0, 0)[1]]
            more = near_sums(table, fops, fine, [box], base, op_ids)[0] if op_ids else 0.0
            near[box] = near_block[box] + more

    def store(at, value):
        near_a[at] = value

    def beside(classes):
        near_side(table, fops, fine_a, rows, cols, 2, 1 - parity("dir"), store, classes)

    widen(strip.at[pl.ds(inside, strip.shape[0] - inside)], fine, 2 * sides)
    widen(side_a, fine_a, 2 * sides)
    zero_box(pat_own)
    zero_box(pat_a)
    boxes = strip.shape[0] // (2 * sides)
    whole = jnp.concatenate([strip[...], side_a[...]], axis=0)
    for j in range(steps + 1):
        if j < steps:
            spread_chunk(whole, interp, j, buffers[j % 2], 2 * sides)
        if j < 2:
            beside(PARITIES[2 * j : 2 * j + 2])
        if j in (2, 3):
            halo(dealt(range(near.shape[0]), j - 2, 2))
        if j:
            buffer = buffers[(j - 1) % 2]
            aggregate_chunk(buffer.at[pl.ds(0, boxes)], trig, j - 1, pat_own, cols, sides)
            aggregate_chunk(buffer.at[pl.ds(boxes, boxes)], trig, j - 1, pat_a, halo_sizes(cols)[0], sides)


def parent_groups(rows, cols):
    return [[(r, c) for r in range(start, rows, 2)] for c in range(cols) for start in range(2)]


def parent_sums(rows, cols, sides, table, pops, sources, index, group, first, width):
    comps = 2 * sides
    rows_at = [4 * rows * cols + r * cols + c for r, c in group]
    sums = [None] * len(group)
    for base, count, ref in sources:
        for t in range(base, base + count):
            op_id = table[5 * rows * cols + 4 + index, t]
            coefs = [row_of(pops, (op_id,), i, first, width, comps) for i in range(2)]
            add_slots(sums, coefs, [ref[table[row, t], :, first : first + width] for row in rows_at])
    return sums


def inner_kernel(rows, cols, sides, table, pat_own, pat_a, *refs):
    *shards, pops, real, imag = refs
    at = 0
    for ref in shards:
        held = ref.shape[3]
        for k in range(ref.shape[0]):
            lane = pl.multiple_of((shard_order("dir")[at] ^ lax.axis_index("dir")) * held, held) if held < pops.shape[2] else 0
            pops[:, :, pl.ds(lane, held)] = ref[k]
            at += 1
    counts = slot_counts(rows, cols, 1)
    at = starts(counts)
    sources = [(at[0], counts[0], pat_own), (at[1], counts[1], pat_a)]
    for first in range(0, real.shape[2], 2 * CHUNK):
        for index, group in enumerate(parent_groups(rows, cols)):
            sums = parent_sums(
                rows, cols, sides, table, pops, sources, index, group, first, 2 * CHUNK
            )
            for (r, c), (re, im) in zip(group, sums):
                real[r * cols + c, :, first : first + 2 * CHUNK] = re
                imag[r * cols + c, :, first : first + 2 * CHUNK] = im


def last_kernel(
    rows, cols, sides,
    table,
    src, interp, trig, fops, pops, real, imag, near_own, near_a,
    out,
    fine, even, odd, pat_b, child, near_b, acc,
):
    comps, fdirs = fine.shape[1:]
    fcols = 2 * cols
    par_counts = slot_counts(rows, cols, 1)
    a_right = 1 - parity("dir")
    steps = interp.shape[1] // CHUNK

    def store(at, value):
        near_b[1 - a_right, at] = value

    def beside():
        near_side(table, fops, fine, rows, cols, 3, 1 - a_right, store, PARITIES)

    def keep():
        for at in range(near_a.shape[0]):
            near_b[a_right, at] = near_a[at]

    def far(j):
        lanes = slice(j * CHUNK, (j + 1) * CHUNK)
        cos, sin = shift_rows(trig, lanes, comps)
        sources = [(starts(par_counts)[2], par_counts[2], pat_b)]
        for index, group in enumerate(parent_groups(rows, cols)):
            sums = parent_sums(rows, cols, sides, table, pops, sources, index, group, j * CHUNK, CHUNK)
            for (r, c), (re, im) in zip(group, sums):
                box = r * cols + c
                total = re + real[box, :, lanes] + times_i(im + imag[box, :, lanes], sides)
                total = total.astype(BF16).astype(F32)
                turned = pltpu.roll(total, sides, 0)
                for k in range(4):
                    at = (2 * r + k // 2) * fcols + 2 * c + k % 2
                    child[at, :, lanes] = (cos[k] * total + sin[k] * turned).astype(BF16)

    def back(j):
        lanes = slice(j * CHUNK, (j + 1) * CHUNK)
        more = lax.dot_general(
            child[:, :, lanes].reshape(-1, CHUNK), interp[:, lanes],
            (((1,), (1,)), ((), ())), preferred_element_type=F32,
        ).reshape(acc.shape)
        acc[...] = more if j == 0 else acc[...] + more

    spread, sums = aggregate_tasks(src, interp, trig, (even, odd), pat_b, halo_sizes(cols)[1], sides)
    plan = [[] for _ in range(steps + 3)]
    for j in range(steps):
        plan[j].append(spread[j])
        plan[j + 1].append(sums[j])
        plan[j + 2].append(functools.partial(far, j))
        plan[min(j + 4, steps + 2) if j + 1 < steps else steps + 2].append(functools.partial(back, j))
    plan[0] += [
        functools.partial(widen, src, fine, comps), functools.partial(zero_box, pat_b), beside, keep,
    ]
    in_steps(plan)

    scale = fdirs / interp.shape[1]
    for r in range(2 * rows):
        for c in range(fcols):
            at = r * fcols + c
            value = near_own[at] + acc[at] * scale
            if c < 2:
                value = value + near_b[0, r * 2 + c]
            if c >= fcols - 2:
                value = value + near_b[1, r * 2 + c - (fcols - 2)]
            out[r, c, 0] = value[:sides]
            out[r, c, 1] = value[sides:]


def per_device(
    fine_out, interp, child_phase, fine_ops, parent_ops, fine_src, fine_op, parent_src, parent_op
):
    frows, fcols, _, sides, fdirs = fine_out.shape
    rows, cols = frows // 2, fcols // 2
    comps = 2 * sides
    pdirs = interp.shape[1]
    assert all(size == cols for size in halo_sizes(cols)) and pdirs % (2 * CHUNK) == 0
    height = rows + sum(halo_sizes(rows))
    boxes = height * cols
    n_dir, bits = lax.axis_size("dir"), swap_bits("dir")

    own = fine_out.reshape(frows * fcols * comps, fdirs)
    outside = boxes - rows * cols
    sources, op_ids, nothing = build_tables(
        rows, cols, {2: [frows * fcols, 4 * outside, 4 * boxes, 4 * boxes], 1: [boxes] * 3}
    )
    ids = shared_ids(op_ids, rows, cols)
    ids = np.pad(ids, [(0, 0), (0, 0), (0, sources.shape[2] - ids.shape[2])])
    nothing = np.broadcast_to(nothing[[0, -1]], (len(PARITIES), 2, nothing.shape[1]))
    lists = jnp.asarray(np.concatenate([sources, op_ids, nothing, ids], axis=1))

    smem = pl.BlockSpec(memory_space=pltpu.SMEM)
    vmem = pl.BlockSpec(memory_space=pltpu.VMEM)

    def shape(*dims):
        return jax.ShapeDtypeStruct(dims, F32)

    def scratch(*dims, kind=F32):
        return pltpu.VMEM(dims, kind)

    def group_scratch(count):
        return [scratch(count + 1, comps, fdirs)] + [scratch(count, comps, CHUNK)] * 2

    def call(body, name, n_smem, outs, scratches, *args):
        return pl.pallas_call(
            functools.partial(body, rows, cols, sides),
            out_shape=outs,
            in_specs=[smem] * n_smem + [vmem] * (len(args) - n_smem),
            out_specs=[vmem] * len(outs),
            scratch_shapes=scratches,
            compiler_params=pltpu.CompilerParams(vmem_limit_bytes=LIMITS.get(name, 4) << 20),
            cost_estimate=pl.CostEstimate(flops=int(COSTS.get(name, 0) * 10**9), bytes_accessed=0, transcendentals=0),
            name=name,
        )(*args)

    near = shape(frows * fcols, comps, fdirs)
    pattern = shape(boxes + 1, comps, pdirs)
    table = call(
        lists_kernel, "lists", 0, [jax.ShapeDtypeStruct((5 * rows * cols + ids.shape[1], ids.shape[2]), jnp.int32)], [],
        fine_op, parent_op, lists,
    )[0]
    first, second = halo_sizes(rows)
    assert first == rows
    edge = call(
        edge_kernel, "edge", 0,
        [jax.ShapeDtypeStruct((own.shape[0] // rows * second, fdirs), BF16)], [], own,
    )[0]
    patch_halo = exchange([own, edge], "patch")
    shards = [parent_ops[None]]
    for bit in reversed(range(bits)):
        held = shards[0]
        if len(shards) > 1:
            count = sum(part.shape[0] for part in shards)
            held = call(hold_kernel, "hold%d" % len(shards), 0, [shape(count, *parent_ops.shape)], [], *shards)[0]
        shards.append(lax.ppermute(held, "dir", [(i, i ^ (1 << bit)) for i in range(n_dir)]))
    near_block, trig = call(
        block_kernel, "block", 1, [near, shape(8, pdirs)], [scratch(frows * fcols + 1, comps, fdirs)],
        table, own, child_phase, fine_ops,
    )
    strip = call(
        pack_kernel, "pack", 0,
        [jax.ShapeDtypeStruct((4 * boxes * comps, fdirs), BF16)], [], own, *patch_halo, near_block,
    )[0]
    side_a, side_b = exchange([strip, strip], "dir")
    if parent_ops.shape[2] % 128:
        shards = [in_order(jnp.concatenate(shards, axis=0), "dir")]
    pat_own, near_own, pat_a, near_a = call(
        both_kernel, "both", 1, [pattern, near, pattern, shape(frows * 2, comps, fdirs)],
        [scratch(4 * outside + 1, comps, fdirs), scratch(4 * boxes + 1, comps, fdirs)] + [scratch(8 * boxes, comps, CHUNK)] * 2,
        table, strip, side_a, interp, trig, fine_ops, near_block,
    )
    part = shape(rows * cols, comps, pdirs)
    pops, real, imag = call(
        inner_kernel, "inner", 1, [shape(parent_ops.shape[0], 2, pdirs), part, part], [],
        table, pat_own, pat_a, *shards,
    )
    return call(
        last_kernel, "last", 1, [jax.ShapeDtypeStruct(fine_out.shape, F32)],
        group_scratch(4 * boxes) + [
            scratch(boxes + 1, comps, pdirs),
            scratch(frows * fcols, comps, pdirs, kind=BF16),
            scratch(2, frows * 2, comps, fdirs),
            scratch(frows * fcols, comps, fdirs),
        ],
        table, side_b, interp, trig, fine_ops, pops, real, imag, near_own, near_a,
    )[0]


def solution(mesh):
    in_specs = (
        P("patch", "dir", None, None, None),
        P(),
        P(),
        P(),
        P(None, None, "dir"),
        P("patch", None, None),
        P("patch", None, None),
        P("patch", None, None),
        P("patch", None, None),
    )
    out_specs = P("patch", "dir", None, None, None)
    return jax.shard_map(
        per_device, mesh=mesh, in_specs=in_specs, out_specs=out_specs, check_vma=False
    )
```

```python
import functools

import jax
import jax.numpy as jnp
import numpy as np
from jax import lax
from jax.experimental import pallas as pl
from jax.experimental.pallas import tpu as pltpu
from jax.sharding import PartitionSpec as P

CHUNK = 512
COSTS = {"hold2": 0.5, "hold3": 0.5, "edge": 0.5}
PIECE = 256
TILE = 8
LIMITS = {"block": 8, "pack": 4, "edge": 4, "lists": 4, "both": 20, "inner": 12, "last": 24}
F32, BF16 = jnp.float32, jnp.bfloat16


def offset_pairs():
    return [(dr, dc) for dr in range(-3, 4) for dc in range(-3, 4) if max(abs(dr), abs(dc)) > 1]


def class_offsets(row_odd, col_odd):
    return [
        (op_id, dr, dc)
        for op_id, (dr, dc) in enumerate(offset_pairs())
        if -2 <= dr + row_odd <= 3 and -2 <= dc + col_odd <= 3
    ]


def halo_sizes(count):
    return (3, 2) if count % 2 else (2, 2)


def stored_at(rel, count, odd):
    first, second = halo_sizes(count)
    if 0 <= rel < count:
        return rel
    if rel < 0:
        return count + first + rel if odd else count + first + second + rel
    return rel if not odd else rel + first


def place(row, col, rows, cols, row_odd, col_odd, scale):
    at_r = stored_at(row // scale, rows, row_odd) * scale + row % scale
    at_c = stored_at(col // scale, cols, col_odd) * scale + col % scale
    for group, width in enumerate((cols, *halo_sizes(cols))):
        if at_c < width * scale:
            return group, at_r * width * scale + at_c
        at_c -= width * scale


def fine_slots(row, col, rows, cols, row_odd, col_odd):
    inside, found = 4 * rows * cols, ([], [], [], [])
    for op_id, dr, dc in class_offsets(row % 2, col % 2):
        group, index = place(row + dr, col + dc, rows, cols, row_odd, col_odd, 2)
        if group:
            found[group + 1].append((op_id, index))
        elif index >= inside:
            found[0].append((op_id, None))
            found[1].append((op_id, index - inside))
        else:
            found[0].append((op_id, index))
    return found


def parent_slots(row, col, rows, cols, row_odd, col_odd):
    found = ([], [], [])
    for op_id, dr, dc in class_offsets((row + row_odd * rows) % 2, (col + col_odd * cols) % 2):
        group, index = place(row + dr, col + dc, rows, cols, row_odd, col_odd, 1)
        found[group].append((op_id, index))
    return found


PARITIES = [(a, b) for a in range(2) for b in range(2)]


def slot_counts(rows, cols, scale):
    slots = fine_slots if scale == 2 else parent_slots
    lists = [
        [len(found) for found in slots(r, c, rows, cols, *odd)]
        for odd in PARITIES for r in range(rows * scale) for c in range(cols * scale)
    ]
    most = [max(column) for column in zip(*lists)]
    return most[:-2] + [max(most[-2:])] * 2


def starts(counts):
    return [sum(counts[:i]) for i in range(len(counts))]


def build_tables(rows, cols, zeros):
    counts = {scale: slot_counts(rows, cols, scale) for scale in (2, 1)}
    width = max(sum(c) for c in counts.values())
    sources, op_ids, nothing = [], [], []
    for odd in PARITIES:
        src_rows, id_rows, none_rows = [], [], []
        for scale, slots in ((2, fine_slots), (1, parent_slots)):
            for r in range(rows * scale):
                for c in range(cols * scale):
                    src_row, id_row, none_row = [], [], []
                    for size, found, zero in zip(counts[scale], slots(r, c, rows, cols, *odd), zeros[scale]):
                        found = found + [(0, None)] * (size - len(found))
                        src_row += [zero if at is None else at for _, at in found]
                        id_row += [o for o, _ in found]
                        none_row += [zero] * size
                    pad = [0] * (width - len(src_row))
                    src_rows.append(src_row + pad)
                    id_rows.append(id_row + pad)
                    none_rows.append(none_row + pad)
        sources.append(src_rows)
        op_ids.append(id_rows)
        nothing = none_rows
    return np.array(sources, np.int32), np.array(op_ids, np.int32), np.array(nothing, np.int32)


def shared_ids(op_ids, rows, cols):
    fine, par = slot_counts(rows, cols, 2), slot_counts(rows, cols, 1)
    width = max(2 * fine[2], sum(par))
    found = []
    for which, (_, dir_odd) in enumerate(PARITIES):
        entries = []
        for a in range(2):
            for c in range(2):
                entry = []
                for group, right in ((2, 1 - dir_odd), (3, dir_odd)):
                    box = a * 2 * cols + right * (2 * cols - 2) + c
                    at = starts(fine)[group]
                    entry += list(op_ids[which, box, at : at + fine[group]])
                entries.append(entry)
        for c in range(cols):
            for start in range(2):
                entries.append(list(op_ids[which, 4 * rows * cols + start * cols + c, : sum(par)]))
        found.append([entry + [0] * (width - len(entry)) for entry in entries])
    return np.array(found, np.int32)


def parity(axis):
    return lax.rem(lax.axis_index(axis), 2)


def parities():
    return parity("patch") * 2 + parity("dir")


def pairs(count, first):
    if first:
        return [(i, i ^ 1) for i in range(count) if (i ^ 1) < count]
    found = []
    for i in range(1, count - 1, 2):
        found += [(i, i + 1), (i + 1, i)]
    return found


def exchange(blocks, axis):
    n = lax.axis_size(axis)
    return [lax.ppermute(block, axis, pairs(n, first)) for block, first in zip(blocks, (True, False))]


def swap_bits(axis):
    return lax.axis_size(axis).bit_length() - 1


def shard_order(axis):
    bits = swap_bits(axis)
    return [int(format(e, "0%db" % bits)[::-1], 2) if bits else 0 for e in range(lax.axis_size(axis))]


def in_order(block, axis):
    n = lax.axis_size(axis)
    at = jnp.asarray(np.array(shard_order(axis), np.int32))[jnp.arange(n, dtype=jnp.int32) ^ lax.axis_index(axis)]
    block = jnp.take(block, at, axis=0)
    return block.transpose(1, 2, 0, 3).reshape(1, block.shape[1], 2, n * block.shape[3])


def times_i(v, sides):
    sign = jnp.where(lax.broadcasted_iota(jnp.int32, (2 * sides, 1), 0) < sides, -1.0, 1.0)
    return sign.astype(F32) * pltpu.roll(v, sides, 0)


def row_of(ref, lead, part, lane, width, comps):
    return jnp.broadcast_to(ref[(*lead, slice(part, part + 1), pl.ds(lane, width))], (comps, width))


def add_slots(sums, coefs, pieces):
    real, imag = coefs
    for m, piece in enumerate(pieces):
        add = [real * piece, imag * piece]
        sums[m] = add if sums[m] is None else [a + b for a, b in zip(sums[m], add)]


def widen(src, fine, comps):
    count = src.shape[0] // comps
    fine[:count] = src[...].astype(F32).reshape(count, comps, src.shape[1])
    fine[count] = jnp.zeros(fine.shape[1:], F32)


def spread_chunk(src, interp, j, buffer, comps):
    lanes = slice(j * CHUNK, (j + 1) * CHUNK)
    out = jnp.dot(src[...], interp[:, lanes], preferred_element_type=F32)
    buffer[...] = out.reshape(-1, comps, CHUNK)


def in_steps(steps):
    for tasks in steps:
        for task in tasks:
            task()


def shift_rows(trig, lanes, comps):
    width = lanes.stop - lanes.start
    sign = jnp.where(lax.broadcasted_iota(jnp.int32, (comps, 1), 0) < comps // 2, 1.0, -1.0).astype(F32)
    rows = [jnp.broadcast_to(trig[k : k + 1, lanes], (comps, width)) for k in range(8)]
    return rows[:4], [sign * row for row in rows[4:]]


def aggregate_chunk(buffer, trig, j, pattern, width, sides):
    comps = 2 * sides
    for at in range(0, CHUNK, PIECE):
        lanes = slice(j * CHUNK + at, j * CHUNK + at + PIECE)
        shift = shift_rows(trig, lanes, comps)
        for q in range(buffer.shape[0] // 4):
            r, c = divmod(q, width)
            total = [None, None]
            for k in range(4):
                piece = buffer[(2 * r + k // 2) * (2 * width) + 2 * c + k % 2, :, at : at + PIECE]
                for i in range(2):
                    add = shift[i][k] * piece
                    total[i] = add if k == 0 else total[i] + add
            whole = total[0] + pltpu.roll(total[1], sides, 0)
            pattern[q, :, lanes] = whole.astype(BF16).astype(F32)


def aggregate_tasks(src, interp, trig, buffers, pattern, width, sides):
    steps = range(interp.shape[1] // CHUNK)
    spread = [
        functools.partial(spread_chunk, src, interp, j, buffers[j % 2], 2 * sides) for j in steps
    ]
    sums = [
        functools.partial(aggregate_chunk, buffers[j % 2], trig, j, pattern, width, sides) for j in steps
    ]
    return spread, sums


def dealt(items, j, steps):
    return items[len(items) * j // steps : len(items) * (j + 1) // steps]


def zero_box(pattern):
    pattern[pattern.shape[0] - 1] = jnp.zeros(pattern.shape[1:], F32)


def near_sums(table, fops, fine, group, base, op_ids):
    comps, fdirs = fine.shape[1:]
    sums = [None] * len(group)
    for t, op_id in enumerate(op_ids, base):
        coefs = [row_of(fops, (op_id,), i, 0, fdirs, comps) for i in range(2)]
        add_slots(sums, coefs, [fine[table[box, t]] for box in group])
    return [real + times_i(imag, comps // 2) for real, imag in sums]


def near_side(table, fops, fine, rows, cols, group, right, store, classes):
    counts = slot_counts(rows, cols, 2)
    base, count = starts(counts)[group], counts[group]
    first_col = right * (2 * cols - 2)
    for a, c in classes:
        boxes = [(2 * r + a) * (2 * cols) + first_col + c for r in range(rows)]
        op_ids = [table[5 * rows * cols + 2 * a + c, (group - 2) * count + t] for t in range(count)]
        for r, value in enumerate(near_sums(table, fops, fine, boxes, base, op_ids)):
            store((2 * r + a) * 2 + c, value)


def block_kernel(rows, cols, sides, table, src, phase, fops, near, trig, fine):
    half = phase.shape[1] // 2
    both = jnp.concatenate([phase[:, :half], phase[:, half:]], axis=0)
    for first, wave in ((0, jnp.cos(both)), (4, jnp.sin(both))):
        trig[first : first + 4, :half] = wave[:4]
        trig[first : first + 4, half:] = wave[4:]
    widen(src, fine, 2 * sides)
    for a in range(2):
        for c in range(2 * cols):
            op_ids = [o for o, _ in fine_slots(a, c, rows, cols, 0, 0)[0]]
            group = [(2 * r + a) * (2 * cols) + c for r in range(rows)]
            for box, value in zip(group, near_sums(table, fops, fine, group, 0, op_ids)):
                near[box] = value


def hold_kernel(rows, cols, sides, *refs):
    *shards, out = refs
    at = 0
    for ref in shards:
        out[at : at + ref.shape[0]] = ref[...]
        at += ref.shape[0]


def lists_kernel(rows, cols, sides, fine_op, par_op, lists, table):
    which = parities()
    at, boxes = 0, 5 * rows * cols
    table[boxes:] = lists[which, 2 * boxes + 2 :]
    for op, scale, none in ((fine_op, 2, 2 * boxes), (par_op, 1, 2 * boxes + 1)):
        across = cols * scale
        assert TILE % across == 0 and op.shape[1] % TILE == 0
        place = lax.axis_index("dir") * across
        first = pl.multiple_of(place // TILE * TILE, TILE)
        for r in range(rows * scale):
            tile = op[r, pl.ds(first, TILE), :]
            mine = tile[:across]
            for skip in range(across, TILE, across):
                mine = jnp.where(lax.rem(place, TILE) == skip, tile[skip : skip + across], mine)
            wanted = lists[which, boxes + at : boxes + at + across]
            found = mine[:, 0:1] == wanted
            for slot in range(1, op.shape[2]):
                found = found | (mine[:, slot : slot + 1] == wanted)
            zero = jnp.broadcast_to(lists[which, none : none + 1], wanted.shape)
            table[at : at + across] = jnp.where(found, lists[which, at : at + across], zero)
            at += across


def edge_kernel(rows, cols, sides, own, edge):
    size = halo_sizes(rows)[1]
    unit = own.shape[0] // rows
    at = pl.multiple_of(parity("patch") * ((rows - size) * unit), unit)
    edge[...] = own[pl.ds(at, size * unit)]


def pack_kernel(rows, cols, sides, own, first, second, after, strip):
    at = 0
    for ref in (own, first, second):
        strip[at : at + ref.shape[0]] = ref[...]
        at += ref.shape[0]


def both_kernel(
    rows, cols, sides, table, strip, side_a, interp, trig, fops, near_block,
    pat_own, near, pat_a, near_a, fine, fine_a, even, odd,
):
    base = starts(slot_counts(rows, cols, 2))[1]
    inside = near.shape[0] * 2 * sides
    buffers = (even, odd)
    steps = interp.shape[1] // CHUNK

    def halo(boxes):
        for box in boxes:
            op_ids = [o for o, _ in fine_slots(*divmod(box, 2 * cols), rows, cols, 0, 0)[1]]
            more = near_sums(table, fops, fine, [box], base, op_ids)[0] if op_ids else 0.0
            near[box] = near_block[box] + more

    def store(at, value):
        near_a[at] = value

    def beside(classes):
        near_side(table, fops, fine_a, rows, cols, 2, 1 - parity("dir"), store, classes)

    widen(strip.at[pl.ds(inside, strip.shape[0] - inside)], fine, 2 * sides)
    widen(side_a, fine_a, 2 * sides)
    zero_box(pat_own)
    zero_box(pat_a)
    boxes = strip.shape[0] // (2 * sides)
    whole = jnp.concatenate([strip[...], side_a[...]], axis=0)
    for j in range(steps + 1):
        if j < steps:
            spread_chunk(whole, interp, j, buffers[j % 2], 2 * sides)
        if j < 2:
            beside(PARITIES[2 * j : 2 * j + 2])
        if j in (2, 3):
            halo(dealt(range(near.shape[0]), j - 2, 2))
        if j:
            buffer = buffers[(j - 1) % 2]
            aggregate_chunk(buffer.at[pl.ds(0, boxes)], trig, j - 1, pat_own, cols, sides)
            aggregate_chunk(buffer.at[pl.ds(boxes, boxes)], trig, j - 1, pat_a, halo_sizes(cols)[0], sides)


def parent_groups(rows, cols):
    return [[(r, c) for r in range(start, rows, 2)] for c in range(cols) for start in range(2)]


def parent_sums(rows, cols, sides, table, pops, sources, index, group, first, width):
    comps = 2 * sides
    rows_at = [4 * rows * cols + r * cols + c for r, c in group]
    sums = [None] * len(group)
    for base, count, ref in sources:
        for t in range(base, base + count):
            op_id = table[5 * rows * cols + 4 + index, t]
            coefs = [row_of(pops, (op_id,), i, first, width, comps) for i in range(2)]
            add_slots(sums, coefs, [ref[table[row, t], :, first : first + width] for row in rows_at])
    return sums


def inner_kernel(rows, cols, sides, table, pat_own, pat_a, *refs):
    *shards, pops, real, imag = refs
    at = 0
    for ref in shards:
        held = ref.shape[3]
        for k in range(ref.shape[0]):
            lane = pl.multiple_of((shard_order("dir")[at] ^ lax.axis_index("dir")) * held, held) if held < pops.shape[2] else 0
            pops[:, :, pl.ds(lane, held)] = ref[k]
            at += 1
    counts = slot_counts(rows, cols, 1)
    at = starts(counts)
    sources = [(at[0], counts[0], pat_own), (at[1], counts[1], pat_a)]
    for first in range(0, real.shape[2], CHUNK):
        for index, group in enumerate(parent_groups(rows, cols)):
            sums = parent_sums(
                rows, cols, sides, table, pops, sources, index, group, first, CHUNK
            )
            for (r, c), (re, im) in zip(group, sums):
                real[r * cols + c, :, first : first + CHUNK] = re
                imag[r * cols + c, :, first : first + CHUNK] = im


def last_kernel(
    rows, cols, sides,
    table,
    src, interp, trig, fops, pops, real, imag, near_own, near_a,
    out,
    fine, even, odd, pat_b, child, near_b, acc,
):
    comps, fdirs = fine.shape[1:]
    fcols = 2 * cols
    par_counts = slot_counts(rows, cols, 1)
    a_right = 1 - parity("dir")
    steps = interp.shape[1] // CHUNK

    def store(at, value):
        near_b[1 - a_right, at] = value

    def beside():
        near_side(table, fops, fine, rows, cols, 3, 1 - a_right, store, PARITIES)

    def keep():
        for at in range(near_a.shape[0]):
            near_b[a_right, at] = near_a[at]

    def far(j):
        lanes = slice(j * CHUNK, (j + 1) * CHUNK)
        cos, sin = shift_rows(trig, lanes, comps)
        sources = [(starts(par_counts)[2], par_counts[2], pat_b)]
        for index, group in enumerate(parent_groups(rows, cols)):
            sums = parent_sums(rows, cols, sides, table, pops, sources, index, group, j * CHUNK, CHUNK)
            for (r, c), (re, im) in zip(group, sums):
                box = r * cols + c
                total = re + real[box, :, lanes] + times_i(im + imag[box, :, lanes], sides)
                total = total.astype(BF16).astype(F32)
                turned = pltpu.roll(total, sides, 0)
                for k in range(4):
                    at = (2 * r + k // 2) * fcols + 2 * c + k % 2
                    child[at, :, lanes] = (cos[k] * total + sin[k] * turned).astype(BF16)

    def back(j):
        lanes = slice(j * CHUNK, (j + 1) * CHUNK)
        more = lax.dot_general(
            child[:, :, lanes].reshape(-1, CHUNK), interp[:, lanes],
            (((1,), (1,)), ((), ())), preferred_element_type=F32,
        ).reshape(acc.shape)
        acc[...] = more if j == 0 else acc[...] + more

    spread, sums = aggregate_tasks(src, interp, trig, (even, odd), pat_b, halo_sizes(cols)[1], sides)
    plan = [[] for _ in range(steps + 3)]
    for j in range(steps):
        plan[j].append(spread[j])
        plan[j + 1].append(sums[j])
        plan[j + 2].append(functools.partial(far, j))
        plan[min(j + 4, steps + 2) if j + 1 < steps else steps + 2].append(functools.partial(back, j))
    plan[0] += [
        functools.partial(widen, src, fine, comps), functools.partial(zero_box, pat_b), beside, keep,
    ]
    in_steps(plan)

    scale = fdirs / interp.shape[1]
    for r in range(2 * rows):
        for c in range(fcols):
            at = r * fcols + c
            value = near_own[at] + acc[at] * scale
            if c < 2:
                value = value + near_b[0, r * 2 + c]
            if c >= fcols - 2:
                value = value + near_b[1, r * 2 + c - (fcols - 2)]
            out[r, c, 0] = value[:sides]
            out[r, c, 1] = value[sides:]


def per_device(
    fine_out, interp, child_phase, fine_ops, parent_ops, fine_src, fine_op, parent_src, parent_op
):
    frows, fcols, _, sides, fdirs = fine_out.shape
    rows, cols = frows // 2, fcols // 2
    comps = 2 * sides
    pdirs = interp.shape[1]
    assert all(size == cols for size in halo_sizes(cols)) and pdirs % (2 * CHUNK) == 0
    height = rows + sum(halo_sizes(rows))
    boxes = height * cols
    n_dir, bits = lax.axis_size("dir"), swap_bits("dir")

    own = fine_out.reshape(frows * fcols * comps, fdirs)
    outside = boxes - rows * cols
    sources, op_ids, nothing = build_tables(
        rows, cols, {2: [frows * fcols, 4 * outside, 4 * boxes, 4 * boxes], 1: [boxes] * 3}
    )
    ids = shared_ids(op_ids, rows, cols)
    ids = np.pad(ids, [(0, 0), (0, 0), (0, sources.shape[2] - ids.shape[2])])
    nothing = np.broadcast_to(nothing[[0, -1]], (len(PARITIES), 2, nothing.shape[1]))
    lists = jnp.asarray(np.concatenate([sources, op_ids, nothing, ids], axis=1))

    smem = pl.BlockSpec(memory_space=pltpu.SMEM)
    vmem = pl.BlockSpec(memory_space=pltpu.VMEM)

    def shape(*dims):
        return jax.ShapeDtypeStruct(dims, F32)

    def scratch(*dims, kind=F32):
        return pltpu.VMEM(dims, kind)

    def group_scratch(count):
        return [scratch(count + 1, comps, fdirs)] + [scratch(count, comps, CHUNK)] * 2

    def call(body, name, n_smem, outs, scratches, *args):
        return pl.pallas_call(
            functools.partial(body, rows, cols, sides),
            out_shape=outs,
            in_specs=[smem] * n_smem + [vmem] * (len(args) - n_smem),
            out_specs=[vmem] * len(outs),
            scratch_shapes=scratches,
            compiler_params=pltpu.CompilerParams(vmem_limit_bytes=LIMITS.get(name, 4) << 20),
            cost_estimate=pl.CostEstimate(flops=int(COSTS.get(name, 0) * 10**9), bytes_accessed=0, transcendentals=0),
            name=name,
        )(*args)

    near = shape(frows * fcols, comps, fdirs)
    pattern = shape(boxes + 1, comps, pdirs)
    table = call(
        lists_kernel, "lists", 0, [jax.ShapeDtypeStruct((5 * rows * cols + ids.shape[1], ids.shape[2]), jnp.int32)], [],
        fine_op, parent_op, lists,
    )[0]
    first, second = halo_sizes(rows)
    assert first == rows
    edge = call(
        edge_kernel, "edge", 0,
        [jax.ShapeDtypeStruct((own.shape[0] // rows * second, fdirs), BF16)], [], own,
    )[0]
    patch_halo = exchange([own, edge], "patch")
    shards = [parent_ops[None]]
    for bit in reversed(range(bits)):
        held = shards[0]
        if len(shards) > 1:
            count = sum(part.shape[0] for part in shards)
            held = call(hold_kernel, "hold%d" % len(shards), 0, [shape(count, *parent_ops.shape)], [], *shards)[0]
        shards.append(lax.ppermute(held, "dir", [(i, i ^ (1 << bit)) for i in range(n_dir)]))
    near_block, trig = call(
        block_kernel, "block", 1, [near, shape(8, pdirs)], [scratch(frows * fcols + 1, comps, fdirs)],
        table, own, child_phase, fine_ops,
    )
    strip = call(
        pack_kernel, "pack", 0,
        [jax.ShapeDtypeStruct((4 * boxes * comps, fdirs), BF16)], [], own, *patch_halo, near_block,
    )[0]
    side_a, side_b = exchange([strip, strip], "dir")
    if parent_ops.shape[2] % 128:
        shards = [in_order(jnp.concatenate(shards, axis=0), "dir")]
    pat_own, near_own, pat_a, near_a = call(
        both_kernel, "both", 1, [pattern, near, pattern, shape(frows * 2, comps, fdirs)],
        [scratch(4 * outside + 1, comps, fdirs), scratch(4 * boxes + 1, comps, fdirs)] + [scratch(8 * boxes, comps, CHUNK)] * 2,
        table, strip, side_a, interp, trig, fine_ops, near_block,
    )
    part = shape(rows * cols, comps, pdirs)
    pops, real, imag = call(
        inner_kernel, "inner", 1, [shape(parent_ops.shape[0], 2, pdirs), part, part], [],
        table, pat_own, pat_a, *shards,
    )
    return call(
        last_kernel, "last", 1, [jax.ShapeDtypeStruct(fine_out.shape, F32)],
        group_scratch(4 * boxes) + [
            scratch(boxes + 1, comps, pdirs),
            scratch(frows * fcols, comps, pdirs, kind=BF16),
            scratch(2, frows * 2, comps, fdirs),
            scratch(frows * fcols, comps, fdirs),
        ],
        table, side_b, interp, trig, fine_ops, pops, real, imag, near_own, near_a,
    )[0]


def solution(mesh):
    in_specs = (
        P("patch", "dir", None, None, None),
        P(),
        P(),
        P(),
        P(None, None, "dir"),
        P("patch", None, None),
        P("patch", None, None),
        P("patch", None, None),
        P("patch", None, None),
    )
    out_specs = P("patch", "dir", None, None, None)
    return jax.shard_map(
        per_device, mesh=mesh, in_specs=in_specs, out_specs=out_specs, check_vma=False
    )
```
